128 devices in a mesh: tm: 8 (over x_lo, y), space: 16 (over z, x_hi, core).
Axes of the slice: x: 4 (x_hi: 2, x_lo: 2; x = x_hi * 2 + x_lo), y: 4, z: 4, core: 2. Of those that a mesh axis runs over, the one named last changes fastest.
Arguments:
- spatial_queries: bfloat16 [1, 16, 1024, 1536], P(None, 'tm', 'space'), may hold values from -40 to 40
- spatial_keys: bfloat16 [1, 16, 1024, 1536], P(None, 'tm', 'space'), may hold values from -40 to 40
- spatial_values: bfloat16 [1, 16, 1024, 1536], P(None, 'tm', 'space'), may hold values from -6 to 6
- temporal_queries: bfloat16 [1, 16, 1024, 1536], P(None, 'tm', 'space'), may hold values from -40 to 40
- temporal_keys: bfloat16 [1, 16, 1024, 1536], P(None, 'tm', 'space'), may hold values from -40 to 40
- temporal_values: bfloat16 [1, 16, 1024, 1536], P(None, 'tm', 'space'), may hold values from -6 to 6
- output_gradient: bfloat16 [1, 16, 1024, 3072], P(None, 'tm', 'space'), may hold values from -6 to 6
- spatial_projection: bfloat16 [1536, 3072], replicated, may hold values from -0.15625 to 0.15625
- temporal_projection: bfloat16 [1536, 3072], replicated, may hold values from -0.15625 to 0.15625
- adapter_down: bfloat16 [1536, 64], replicated, may hold values from -0.15625 to 0.15625
- adapter_up: bfloat16 [64, 3072], replicated, may hold values from -0.75 to 0.75
- spatial_channel_gate: float32 [3072], replicated, may hold values from 0.25 to 1.5
- temporal_channel_gate: float32 [3072], replicated, may hold values from 0.25 to 1.5
Outputs:
- grad_q_spatial: bfloat16 [1, 16, 1024, 1536], P(None, 'tm', 'space')
- grad_k_spatial: bfloat16 [1, 16, 1024, 1536], P(None, 'tm', 'space')
- grad_v_spatial: bfloat16 [1, 16, 1024, 1536], P(None, 'tm', 'space')
- grad_q_temporal: bfloat16 [1, 16, 1024, 1536], P(None, 'tm', 'space')
- grad_k_temporal: bfloat16 [1, 16, 1024, 1536], P(None, 'tm', 'space')
- grad_v_temporal: bfloat16 [1, 16, 1024, 1536], P(None, 'tm', 'space')
- grad_lora_down: float32 [1536, 64], replicated
- grad_lora_up: float32 [64, 3072], replicated
- grad_gate_spatial: float32 [3072], replicated
- grad_gate_temporal: float32 [3072], replicated
The draws below stay inside these ranges and needn't reach their ends.
All inputs are finite; a program needn't handle non-finite values.
Results may differ from the reference program's by a relative error of at most 0.034.
Values may be sent and summed in bfloat16 or wider, within the bound.
A program may use at most 192 MiB of HBM per device.

```python
import jax
import jax.numpy as jnp
from jax import lax

MODEL_WIDTH = 3072
LOCAL_HEADS = 12
HEAD_FEATURES = 128
ADAPTER_RANK = 64
BATCH = 1
FRAMES = 16
PATCHES = 1024
N_TM = 8
N_SPACE = 16


def pair_fields(key, field_shape, along_axis):
    subkeys = jax.random.split(key, 5)
    query = jax.random.normal(subkeys[0], field_shape, jnp.float32)
    key_field = jax.random.normal(subkeys[1], field_shape, jnp.float32)
    base_field = jax.random.normal(subkeys[2], field_shape, jnp.float32)
    noise_field = jax.random.normal(subkeys[3], field_shape, jnp.float32)
    strength = jax.random.uniform(subkeys[4], field_shape[:-1] + (1,), jnp.float32, 3.0, 6.0)
    spot_field = base_field * strength
    shifted = jnp.roll(spot_field, 1, axis=along_axis)
    position = lax.broadcasted_iota(jnp.int32, field_shape, along_axis)
    lead_rows = position % 8 == 0
    follow = position % 8 == 1
    strong_query = jnp.where(lead_rows, spot_field, query)
    strong_key = jnp.where(lead_rows, spot_field, jnp.where(follow, shifted + 0.4 * noise_field, key_field))
    return (query, key_field, strong_query, strong_key)


def draw_spatial_queries(key, part):
    fields = pair_fields(key, (BATCH, FRAMES, PATCHES, LOCAL_HEADS * HEAD_FEATURES), 2)
    return fields[0].astype(jnp.bfloat16)


def draw_spatial_keys(key, part):
    fields = pair_fields(key, (BATCH, FRAMES, PATCHES, LOCAL_HEADS * HEAD_FEATURES), 2)
    return fields[1].astype(jnp.bfloat16)


def draw_temporal_queries(key, part):
    fields = pair_fields(jax.random.fold_in(key, 7), (BATCH, FRAMES, PATCHES, LOCAL_HEADS * HEAD_FEATURES), 1)
    return fields[0].astype(jnp.bfloat16)


def draw_temporal_keys(key, part):
    fields = pair_fields(jax.random.fold_in(key, 7), (BATCH, FRAMES, PATCHES, LOCAL_HEADS * HEAD_FEATURES), 1)
    return fields[1].astype(jnp.bfloat16)


def block_scale(rng, extent, cuts, low, top_value):
    gain, own = 1.0, jax.random.fold_in(rng, 6)
    for axis_at, blocks in cuts:
        draws = jnp.exp(jax.random.uniform(jax.random.fold_in(own, axis_at), (blocks,), jnp.float32, low / len(cuts), top_value / len(cuts)))
        gain = gain * jnp.repeat(draws, extent[axis_at] // blocks).reshape([-1 if axis == axis_at else 1 for axis in range(len(extent))])
    return gain


def gaussian(own_key, extent, deviation, bound, pieces=(), held_as=jnp.bfloat16):
    array = jax.random.normal(own_key, extent, jnp.float32) * deviation
    if len(pieces) > 0:
        array = block_scale(own_key, extent, pieces, -0.22, 0.18) * array
    return jnp.clip(array, min=-bound, max=bound).astype(held_as)


def setup_inputs(seed: int = 0) -> dict:
    key_of = jax.random.split(jax.random.key(seed), 14)
    spatial_queries = draw_spatial_queries(jax.random.fold_in(key_of[13], 71), 0)
    spatial_keys = draw_spatial_keys(jax.random.fold_in(key_of[13], 71), 0)
    spatial_values = gaussian(key_of[2], (BATCH, FRAMES, PATCHES, LOCAL_HEADS * HEAD_FEATURES), 1.0, 6.0, ((1, 8), (2, 16)))
    temporal_queries = draw_temporal_queries(jax.random.fold_in(key_of[13], 71), 0)
    temporal_keys = draw_temporal_keys(jax.random.fold_in(key_of[13], 71), 0)
    temporal_values = gaussian(key_of[5], (BATCH, FRAMES, PATCHES, LOCAL_HEADS * HEAD_FEATURES), 1.0, 6.0, ((1, 8), (2, 16)))
    output_gradient = gaussian(key_of[6], (BATCH, FRAMES, PATCHES, MODEL_WIDTH), 1.0, 6.0, ((1, 8), (2, 16)))
    spatial_projection = gaussian(key_of[7], (LOCAL_HEADS * HEAD_FEATURES, MODEL_WIDTH), (LOCAL_HEADS * HEAD_FEATURES) ** -0.5, 0.15625)
    temporal_projection = gaussian(key_of[8], (LOCAL_HEADS * HEAD_FEATURES, MODEL_WIDTH), (LOCAL_HEADS * HEAD_FEATURES) ** -0.5, 0.15625)
    adapter_down = gaussian(key_of[9], (LOCAL_HEADS * HEAD_FEATURES, ADAPTER_RANK), (LOCAL_HEADS * HEAD_FEATURES) ** -0.5, 0.15625)
    adapter_up = gaussian(key_of[10], (ADAPTER_RANK, MODEL_WIDTH), ADAPTER_RANK ** -0.5, 0.75)
    spatial_channel_gate = jnp.clip(jax.random.uniform(key_of[11], (MODEL_WIDTH,), jnp.float32, 0.25, 1.5), 0.25, 1.5)
    temporal_channel_gate = jnp.clip(jax.random.uniform(key_of[12], (MODEL_WIDTH,), jnp.float32, 0.25, 1.5), 0.25, 1.5)
    return dict(spatial_queries=spatial_queries, spatial_keys=spatial_keys, spatial_values=spatial_values, temporal_queries=temporal_queries, temporal_keys=temporal_keys, temporal_values=temporal_values, output_gradient=output_gradient, spatial_projection=spatial_projection, temporal_projection=temporal_projection, adapter_down=adapter_down, adapter_up=adapter_up, spatial_channel_gate=spatial_channel_gate, temporal_channel_gate=temporal_channel_gate)


def split_heads(tensor, temporal_pass):
    batch_count, frames, patches, feat_width = tensor.shape
    tensor = tensor.reshape(batch_count, frames, patches, LOCAL_HEADS, HEAD_FEATURES)
    if temporal_pass:
        return tensor.transpose(0, 2, 3, 1, 4).reshape(batch_count * patches * LOCAL_HEADS, frames, HEAD_FEATURES)
    return tensor.transpose(0, 1, 3, 2, 4).reshape(batch_count * frames * LOCAL_HEADS, patches, HEAD_FEATURES)


def join_heads(tensor, temporal_pass, batch_count, frames, patches):
    if temporal_pass:
        tensor = tensor.reshape(batch_count, patches, LOCAL_HEADS, frames, HEAD_FEATURES).transpose(0, 3, 1, 2, 4)
    else:
        tensor = tensor.reshape(batch_count, frames, LOCAL_HEADS, patches, HEAD_FEATURES).transpose(0, 1, 3, 2, 4)
    return tensor.reshape(batch_count, frames, patches, LOCAL_HEADS * HEAD_FEATURES)


def in_blocks(function, arrays):
    shaped = tuple(item.reshape((-1, LOCAL_HEADS) + item.shape[1:]) for item in arrays)
    results = lax.map(lambda items: function(*items), shaped)
    return tuple(item.reshape((-1,) + item.shape[2:]) for item in results)


def attend(queries, key_items, value_items):
    head_scale = HEAD_FEATURES ** -0.5
    scores = jnp.einsum("nqe,nke->nqk", queries.astype(jnp.float32), key_items.astype(jnp.float32)) * head_scale
    row_max = jnp.max(scores, axis=-1, keepdims=True)
    exp_scores = jnp.exp(scores - row_max)
    row_sum = jnp.sum(exp_scores, axis=-1, keepdims=True)
    prob_low = (exp_scores / row_sum).astype(jnp.bfloat16)
    attended = jnp.einsum("nqk,nke->nqe", prob_low.astype(jnp.float32), value_items.astype(jnp.float32))
    return attended.astype(jnp.bfloat16), row_max + jnp.log(row_sum)


def attend_back(queries, key_items, value_items, attended, log_norm, grad_attended, head_groups):
    head_scale = HEAD_FEATURES ** -0.5
    query_wide = queries.astype(jnp.float32)
    grad_wide = grad_attended.astype(jnp.float32)
    scores = jnp.einsum("nqe,nke->nqk", query_wide, key_items.astype(jnp.float32)) * head_scale
    prob_back = jnp.exp(scores - log_norm)
    row_dot = jnp.sum(grad_wide * attended.astype(jnp.float32), axis=-1, keepdims=True)
    grad_probs = jnp.einsum("nqe,nke->nqk", grad_wide, value_items.astype(jnp.float32))
    grad_scores = (prob_back * (grad_probs - row_dot)).astype(jnp.bfloat16)
    prob_low = prob_back.astype(jnp.bfloat16)
    grad_query = jnp.einsum("nqk,nke->nqe", grad_scores.astype(jnp.float32), key_items.astype(jnp.float32)) * head_scale
    group_rows = queries.shape[1] // head_groups
    empty_sum = jnp.zeros(key_items.shape, jnp.float32)

    def add_group(running, group_index):
        row_start = (group_index * group_rows).astype(jnp.int32)
        part_scores = lax.dynamic_slice_in_dim(grad_scores, row_start, group_rows, 1).astype(jnp.float32)
        part_probs = lax.dynamic_slice_in_dim(prob_low, row_start, group_rows, 1).astype(jnp.float32)
        part_query = lax.dynamic_slice_in_dim(query_wide, row_start, group_rows, 1)
        part_grad = lax.dynamic_slice_in_dim(grad_wide, row_start, group_rows, 1)
        key_part = jnp.einsum("nqk,nqe->nke", part_scores, part_query) * head_scale
        value_part = jnp.einsum("nqk,nqe->nke", part_probs, part_grad)
        key_part = lax.optimization_barrier(key_part.astype(jnp.bfloat16)).astype(jnp.float32)
        value_part = lax.optimization_barrier(value_part.astype(jnp.bfloat16)).astype(jnp.float32)
        return (running[0] + key_part, running[1] + value_part), None

    sums, unused = lax.scan(add_group, (empty_sum, empty_sum), jnp.arange(head_groups, dtype=jnp.int32))
    return grad_query.astype(jnp.bfloat16), sums[0].astype(jnp.bfloat16), sums[1].astype(jnp.bfloat16)


def adapter_branch(attention_rows, gradient_rows, projection_weight, adapter_down, adapter_up, gate_vector):
    lowrank_state = jnp.dot(attention_rows, adapter_down, preferred_element_type=jnp.float32).astype(jnp.bfloat16)
    branch_output = jnp.dot(attention_rows, projection_weight, preferred_element_type=jnp.float32) + jnp.dot(lowrank_state, adapter_up, preferred_element_type=jnp.float32)
    grad_wide = gradient_rows.astype(jnp.float32)
    gate_gradient = jnp.sum(grad_wide * branch_output, axis=0)
    branch_gradient = (grad_wide * gate_vector).astype(jnp.bfloat16)
    lowrank_gradient = jnp.dot(branch_gradient, adapter_up.T, preferred_element_type=jnp.float32).astype(jnp.bfloat16)
    up_gradient = jnp.dot(lowrank_state.T, branch_gradient, preferred_element_type=jnp.float32)
    down_gradient = jnp.dot(attention_rows.T, lowrank_gradient, preferred_element_type=jnp.float32)
    attention_gradient = jnp.dot(branch_gradient, projection_weight.T, preferred_element_type=jnp.float32) + jnp.dot(lowrank_gradient, adapter_down.T, preferred_element_type=jnp.float32)
    return attention_gradient.astype(jnp.bfloat16), down_gradient, up_gradient, gate_gradient


def single_block(input_queries, input_keys, input_values, output_gradient, projection_weight, adapter_down, adapter_up, gate_vector, temporal_pass, head_groups):
    batch_count, frames, patches, feat_width = input_queries.shape
    queries = split_heads(input_queries, temporal_pass)
    key_items = split_heads(input_keys, temporal_pass)
    value_items = split_heads(input_values, temporal_pass)
    attended, log_norm = in_blocks(attend, (queries, key_items, value_items))
    attention_rows = join_heads(attended, temporal_pass, batch_count, frames, patches).reshape(-1, LOCAL_HEADS * HEAD_FEATURES)
    gradient_rows = output_gradient.reshape(-1, output_gradient.shape[-1])
    attention_gradient, down_gradient, up_gradient, gate_gradient = adapter_branch(attention_rows, gradient_rows, projection_weight, adapter_down, adapter_up, gate_vector)
    grad_items = split_heads(attention_gradient.reshape(batch_count, frames, patches, LOCAL_HEADS * HEAD_FEATURES), temporal_pass)

    def back_block(part_q, part_k, part_v, part_att, part_norm, part_grad):
        return attend_back(part_q, part_k, part_v, part_att, part_norm, part_grad, head_groups)

    grad_query, grad_key, grad_value = in_blocks(back_block, (queries, key_items, value_items, attended, log_norm, grad_items))
    grads = (join_heads(grad_query, temporal_pass, batch_count, frames, patches), join_heads(grad_key, temporal_pass, batch_count, frames, patches), join_heads(grad_value, temporal_pass, batch_count, frames, patches))
    return grads, down_gradient, up_gradient, gate_gradient


def reference(spatial_queries, spatial_keys, spatial_values, temporal_queries, temporal_keys, temporal_values, output_gradient, spatial_projection, temporal_projection, adapter_down, adapter_up, spatial_channel_gate, temporal_channel_gate):
    spatial_gradients, down_spatial, up_spatial, gate_space = single_block(spatial_queries, spatial_keys, spatial_values, output_gradient, spatial_projection, adapter_down, adapter_up, spatial_channel_gate, False, N_SPACE)
    temporal_gradients, down_temporal, up_temporal, gate_time = single_block(temporal_queries, temporal_keys, temporal_values, output_gradient, temporal_projection, adapter_down, adapter_up, temporal_channel_gate, True, N_TM)
    return (spatial_gradients[0], spatial_gradients[1], spatial_gradients[2], temporal_gradients[0], temporal_gradients[1], temporal_gradients[2], down_spatial + down_temporal, up_spatial + up_temporal, gate_space, gate_time)
```

```python
import jax
import jax.numpy as jnp
from jax import lax
from jax.experimental import pallas as pl
from jax.experimental.pallas import tpu as pltpu
from jax.sharding import PartitionSpec as P

MESH = pl.DeviceIdType.MESH
BF = jnp.bfloat16
F32 = jnp.float32
SCALE = 128 ** (-0.5)
NN = (((1,), (0,)), ((), ()))
NT = (((1,), (1,)), ((), ()))
TN = (((0,), (0,)), ((), ()))
ROWS = 2688
PART = 336
PIECE = 24


def dot(a, b, dims):
    return lax.dot_general(a, b, dims, preferred_element_type=F32)


def aligned(value, unit):
    return pl.multiple_of(value, unit)


def kernel(
    sq, sk, sv, tq, tk, tv, og_hbm, ws_hbm, wt_hbm, down_hbm, up_hbm, gs_hbm, gt_hbm,
    o_sq, o_sk, o_sv, o_tq, o_tk, o_tv, o_down, o_up, o_gs, o_gt,
    sr, so, prob, dsc, tr, to, og, ws, wt, down, up, gs, gt, gb, glow, ga_s, ga_t, ah_s, ah_t,
    low, gate_rows, pr, r1, acc, r2, s2, r3, b4, r4,
    load_sem, s_in, s_out, t_in, t_out, s_home, s_back, t_home, t_back, red_in, red_out,
):
    t = lax.axis_index("tm")
    s = lax.axis_index("space")
    chip = s // 2
    core = lax.rem(s, 2)
    z = s // 4
    xh = lax.rem(chip, 2)
    ia = z * 2 + core
    ib = xh * 8 + t

    loads = [
        pltpu.make_async_copy(src, dst, load_sem.at[n])
        for n, (src, dst) in enumerate(
            ((og_hbm, og), (gs_hbm, gs), (gt_hbm, gt), (up_hbm, up), (down_hbm, down), (ws_hbm, ws), (wt_hbm, wt))
        )
    ]
    for load in loads:
        load.start()

    gate = pltpu.get_barrier_semaphore()

    def greet(device):
        pl.semaphore_signal(gate, inc=1, device_id=device, device_id_type=MESH)

    def greet_space(n, carry):
        greet((t, lax.rem(s + n, 16)))
        return carry

    def greet_tm(n, carry):
        other = lax.rem(t + n, 8)
        greet((other, s))
        greet((other, z * 4 + (1 - xh) * 2 + core))
        return carry

    lax.fori_loop(1, 16, greet_space, 0)
    lax.fori_loop(1, 8, greet_tm, 0)
    pl.semaphore_wait(gate, 29)

    def start_local(src, dst, sem):
        pltpu.make_async_copy(src, dst, sem).start()

    def start_remote(src, dst, send, recv, device):
        pltpu.make_async_remote_copy(
            src, dst, send, recv, device_id=device, device_id_type=MESH
        ).start()

    def await_bytes(ref, sem):
        pltpu.make_async_copy(ref, ref, sem).wait()

    WIDTH = (256, 128)

    def spatial_out(src, i):
        def ends(d, k):
            col = aligned(lax.rem(d, 4) * 384 + k * 256, 128)
            return (
                src.at[d // 4, :, pl.ds(col, WIDTH[k])],
                sr.at[i, pl.ds(aligned(s * 64, 64), 64), pl.ds(0, WIDTH[k])],
            )

        def step(n, carry):
            d = lax.rem(chip + n, 8)
            for k in (0, 1):
                a, b = ends(d, k)
                start_remote(a, b, s_out.at[i], s_in.at[i], (t, d * 2 + k))
            return carry

        lax.fori_loop(1, 8, step, 0)
        for k in (0, 1):
            a, b = ends(chip, k)

            @pl.when(core == k)
            def _():
                start_local(a, b, s_in.at[i])

            @pl.when(core != k)
            def _():
                start_remote(a, b, s_out.at[i], s_in.at[i], (t, chip * 2 + k))

    def spatial_arrived(i):
        @pl.when(core == 0)
        def _():
            await_bytes(sr.at[i], s_in.at[i])

        @pl.when(core == 1)
        def _():
            await_bytes(sr.at[i, :, pl.ds(0, 128)], s_in.at[i])

    def spatial_back(j, home):
        for k in (0, 1):

            @pl.when(core == k)
            def _():
                col = aligned(lax.rem(chip, 4) * 384 + k * 256, 128)
                dst = home.at[chip // 4, :, pl.ds(col, WIDTH[k])]

                def src(d):
                    return so.at[j, pl.ds(aligned(d * 64, 64), 64), pl.ds(0, WIDTH[k])]

                def step(n, carry):
                    d = lax.rem(s + n, 16)
                    start_remote(src(d), dst, s_back.at[j], s_home.at[j], (t, d))
                    return carry

                lax.fori_loop(1, 16, step, 0)
                start_local(src(s), dst, s_home.at[j])

    def temporal_out(src, i):
        def ends(d):
            row = aligned(lax.rem(d, 4) * 16, 16)
            col = aligned((d // 4) * 768, 128)
            return src.at[:, pl.ds(row, 16), pl.ds(col, 768)], tr.at[i, pl.ds(2 * t, 2)]

        def step(n, carry):
            d = lax.rem(t + n, 8)
            a, b = ends(d)
            start_remote(a, b, t_out.at[i], t_in.at[i], (d, s))
            return carry

        lax.fori_loop(1, 8, step, 0)
        a, b = ends(t)
        start_local(a, b, t_in.at[i])

    def temporal_back(j, home):
        row = aligned(lax.rem(t, 4) * 16, 16)
        col = aligned((t // 4) * 768, 128)
        dst = home.at[:, pl.ds(row, 16), pl.ds(col, 768)]

        def step(n, carry):
            d = lax.rem(t + n, 8)
            start_remote(to.at[j, pl.ds(2 * d, 2)], dst, t_back.at[j], t_home.at[j], (d, s))
            return carry

        lax.fori_loop(1, 8, step, 0)
        start_local(to.at[j, pl.ds(2 * t, 2)], dst, t_home.at[j])

    for i, src in enumerate((sq, sk, sv)):
        spatial_out(src, i)

    def attention_gradient(b, channel_gate, weight, weight_load, home):
        branch = (og[...].astype(F32) * channel_gate[...]).astype(BF)
        gb[b] = branch
        small = dot(branch, up[...], NT).astype(BF)
        glow[b] = small
        weight_load.wait()

        def step(n, carry):
            rows = pl.ds(aligned(n * 256, 256), 256)
            part = dot(gb[b], weight[rows, :], NT) + dot(small, down[rows, :], NT)
            home[:, :, rows] = part.astype(BF).reshape(2, 64, 256)
            return carry

        lax.fori_loop(0, 6, step, 0)

    for load in loads[:5]:
        load.wait()
    attention_gradient(0, gs, ws, loads[5], ga_s)
    spatial_out(ga_s, 3)
    for i, src in enumerate((tq, tk, tv)):
        temporal_out(src, i)
    attention_gradient(1, gt, wt, loads[6], ga_t)
    temporal_out(ga_t, 3)

    heads = 2 - core
    for i in range(3):
        spatial_arrived(i)

    def spatial_forward(h, carry):
        c = pl.ds(aligned(h * 128, 128), 128)
        keys = sr[1, :, c]
        values = sr[2, :, c]
        for n in range(4):
            r = pl.ds(n * 256, 256)
            scores = dot(sr[0, r, c], keys, NT) * SCALE
            expd = jnp.exp(scores - jnp.max(scores, axis=1, keepdims=True))
            total = jnp.sum(expd, axis=1, keepdims=True)
            low_prob = (expd * (1.0 / total)).astype(BF)
            prob[h, r, :] = low_prob
            so[0, r, c] = dot(low_prob, values, NN).astype(BF)
        return carry

    lax.fori_loop(0, heads, spatial_forward, 0)
    spatial_back(0, ah_s)

    spatial_arrived(3)

    def spatial_backward(h, carry):
        c = pl.ds(aligned(h * 128, 128), 128)
        keys = sr[1, :, c]
        values = sr[2, :, c]
        for n in range(4):
            r = pl.ds(n * 256, 256)
            grad = sr[3, r, c]
            row_dot = jnp.sum(
                grad.astype(F32) * so[0, r, c].astype(F32), axis=1, keepdims=True
            )
            grad_prob = dot(grad, values, NT)
            grad_scores = (prob[h, r, :].astype(F32) * (grad_prob - row_dot)).astype(BF)
            dsc[r, :] = grad_scores
            so[1, r, c] = (dot(grad_scores, keys, NN) * SCALE).astype(BF)
        queries_t = sr[0, :, c].T
        grads_t = sr[3, :, c].T
        for n in range(4):
            r = pl.ds(n * 256, 256)
            so[2, r, c] = (dot(queries_t, dsc[:, r], NN) * SCALE).T.astype(BF)
            so[3, r, c] = dot(grads_t, prob[h, :, r], NN).T.astype(BF)
        return carry

    lax.fori_loop(0, heads, spatial_backward, 0)
    for j, home in ((1, o_sq), (2, o_sk), (3, o_sv)):
        spatial_back(j, home)

    for i in range(4):
        await_bytes(tr.at[i], t_in.at[i])
    same_patch = lax.rem(lax.broadcasted_iota(jnp.int32, (256, 256), 0), 16) == lax.rem(
        lax.broadcasted_iota(jnp.int32, (256, 256), 1), 16
    )

    def temporal_head(h, carry):
        c = pl.ds(aligned(h * 128, 128), 128)
        queries, keys, values, grad = (tr[i, :, :, c].reshape(256, 128) for i in range(4))
        scores = jnp.where(same_patch, dot(queries, keys, NT) * SCALE, -1e30)
        expd = jnp.exp(scores - jnp.max(scores, axis=1, keepdims=True))
        total = jnp.sum(expd, axis=1, keepdims=True)
        probs = expd * (1.0 / total)
        low_prob = probs.astype(BF)
        attended = dot(low_prob, values, NN).astype(BF)
        row_dot = jnp.sum(grad.astype(F32) * attended.astype(F32), axis=1, keepdims=True)
        grad_scores = (probs * (dot(grad, values, NT) - row_dot)).astype(BF)
        out = (
            attended,
            (dot(grad_scores, keys, NN) * SCALE).astype(BF),
            (dot(grad_scores, queries, TN) * SCALE).astype(BF),
            dot(low_prob, grad, TN).astype(BF),
        )
        for j in range(4):
            to[j, :, :, c] = out[j].reshape(16, 16, 128)
        return carry

    lax.fori_loop(0, 6, temporal_head, 0)
    for j, home in ((0, ah_t), (1, o_tq), (2, o_tk), (3, o_tv)):
        temporal_back(j, home)

    def adapter(b, home, arrived, weight):
        await_bytes(home, arrived)
        rows = home[...].reshape(128, 1536)
        small = dot(rows, down[...], NN).astype(BF)
        low[b] = small

        def step(n, carry):
            c = pl.ds(aligned(n * 512, 512), 512)
            branch = dot(home[...].reshape(128, 1536), weight[:, c], NN) + dot(low[b], up[:, c], NN)
            gate_rows[b, :, c] = jnp.sum(og[:, c].astype(F32) * branch, axis=0, keepdims=True)
            return carry

        lax.fori_loop(0, 6, step, 0)

    adapter(0, ah_s, s_home.at[0], ws)
    adapter(1, ah_t, t_home.at[0], wt)

    low_st = low[0].astype(F32).T.astype(BF)
    low_tt = low[1].astype(F32).T.astype(BF)
    glow_st = glow[0].astype(F32).T.astype(BF)
    glow_tt = glow[1].astype(F32).T.astype(BF)
    line = lax.broadcasted_iota(jnp.int32, (16, 128), 0)
    for j in range(24):
        c = pl.ds(j * 128, 128)
        pr[pl.ds(j * 80, 64), :] = (
            dot(low_st, gb[0, :, c], NN) + dot(low_tt, gb[1, :, c], NN)
        ).astype(BF)
        pr[pl.ds(j * 80 + 64, 16), :] = jnp.where(
            line == 0, gate_rows[0, :, c], jnp.where(line == 1, gate_rows[1, :, c], 0.0)
        ).astype(BF)
    for j in range(12):
        c = pl.ds(j * 128, 128)
        pr[pl.ds(1920 + j * 64, 64), :] = (
            dot(glow_st, ah_s[:, :, c].reshape(128, 128), NN)
            + dot(glow_tt, ah_t[:, :, c].reshape(128, 128), NN)
        ).astype(BF)

    def in_a(j):
        return (t, (j // 2) * 4 + xh * 2 + lax.rem(j, 2))

    def in_b(j):
        return (lax.rem(j, 8), z * 4 + (j // 8) * 2 + core)

    def exchange(stage, size, mine, device, src, dst):
        def step(n, carry):
            j = lax.rem(mine + n, size)
            start_remote(src(j), dst, red_out.at[stage], red_in.at[stage], device(j))
            return carry

        lax.fori_loop(1, size, step, 0)
        start_local(src(mine), dst, red_in.at[stage])

    exchange(
        0, 8, ia, in_a,
        lambda j: pr.at[pl.ds(aligned(j * PART, 16), PART), :],
        r1.at[ia],
    )
    await_bytes(r1, red_in.at[0])
    total = r1[0].astype(F32)
    for n in range(1, 8):
        total = total + r1[n].astype(F32)
    acc[pl.ds(0, PART), :] = total
    acc[pl.ds(PART, 16 * PIECE - PART), :] = jnp.zeros((16 * PIECE - PART, 128), F32)

    exchange(
        1, 16, ib, in_b,
        lambda j: acc.at[pl.ds(aligned(j * PIECE, 8), PIECE), :],
        r2.at[ib],
    )
    await_bytes(r2, red_in.at[1])
    total = r2[0]
    for n in range(1, 16):
        total = total + r2[n]
    s2[...] = total

    exchange(2, 16, ib, in_b, lambda j: s2, r3.at[pl.ds(aligned(ib * PIECE, 8), PIECE), :])
    await_bytes(r3, red_in.at[2])
    b4[...] = r3[pl.ds(0, PART), :].astype(BF)

    exchange(3, 8, ia, in_a, lambda j: b4, r4.at[pl.ds(aligned(ia * PART, 16), PART), :])
    await_bytes(r4, red_in.at[3])
    for j in range(24):
        c = pl.ds(j * 128, 128)
        o_up[:, c] = r4[pl.ds(j * 80, 64), :].astype(F32)
        tail = r4[pl.ds(j * 80 + 64, 16), :].astype(F32)
        o_gs[:, c] = tail[0:1]
        o_gt[:, c] = tail[1:2]
    for j in range(12):
        o_down[pl.ds(j * 128, 128), :] = r4[pl.ds(1920 + j * 64, 64), :].astype(F32).T

    for j, (s_ref, t_ref) in enumerate(((None, None), (o_sq, o_tq), (o_sk, o_tk), (o_sv, o_tv))):
        if j > 0:
            await_bytes(s_ref, s_home.at[j])
            await_bytes(t_ref, t_home.at[j])
    for i in range(4):
        await_bytes(tr.at[0, pl.ds(0, 14)], t_out.at[i])
        await_bytes(to.at[0, pl.ds(0, 14)], t_back.at[i])
        for k in (0, 1):

            @pl.when(core == k)
            def _():
                await_bytes(og.at[pl.ds(0, 64), pl.ds(0, 3072 - WIDTH[k])], s_out.at[i])
                await_bytes(so.at[0, pl.ds(0, 960), pl.ds(0, WIDTH[k])], s_back.at[i])

    await_bytes(pr.at[pl.ds(0, 7 * PART), :], red_out.at[0])
    await_bytes(acc.at[pl.ds(0, 15 * PIECE), :], red_out.at[1])
    await_bytes(acc.at[pl.ds(0, 15 * PIECE), :], red_out.at[2])
    await_bytes(pr.at[pl.ds(0, 7 * PART), :], red_out.at[3])


def shards(
    spatial_queries,
    spatial_keys,
    spatial_values,
    temporal_queries,
    temporal_keys,
    temporal_values,
    output_gradient,
    spatial_projection,
    temporal_projection,
    adapter_down,
    adapter_up,
    spatial_channel_gate,
    temporal_channel_gate,
):
    tokens = jax.ShapeDtypeStruct((2, 64, 1536), BF)
    dma = pltpu.SemaphoreType.DMA
    outs = pl.pallas_call(
        kernel,
        out_shape=(tokens,) * 6
        + (
            jax.ShapeDtypeStruct((1536, 64), F32),
            jax.ShapeDtypeStruct((64, 3072), F32),
            jax.ShapeDtypeStruct((1, 3072), F32),
            jax.ShapeDtypeStruct((1, 3072), F32),
        ),
        in_specs=[pl.BlockSpec(memory_space=pl.ANY)] * 13,
        out_specs=[pl.BlockSpec(memory_space=pl.ANY)] * 6
        + [pl.BlockSpec(memory_space=pltpu.VMEM)] * 4,
        scratch_shapes=[
            pltpu.VMEM((4, 1024, 256), BF),
            pltpu.VMEM((4, 1024, 256), BF),
            pltpu.VMEM((2, 1024, 1024), BF),
            pltpu.VMEM((1024, 1024), BF),
            pltpu.VMEM((4, 16, 16, 768), BF),
            pltpu.VMEM((4, 16, 16, 768), BF),
            pltpu.VMEM((128, 3072), BF),
            pltpu.VMEM((1536, 3072), BF),
            pltpu.VMEM((1536, 3072), BF),
            pltpu.VMEM((1536, 64), BF),
            pltpu.VMEM((64, 3072), BF),
            pltpu.VMEM((1, 3072), F32),
            pltpu.VMEM((1, 3072), F32),
            pltpu.VMEM((2, 128, 3072), BF),
            pltpu.VMEM((2, 128, 64), BF),
            pltpu.VMEM((2, 64, 1536), BF),
            pltpu.VMEM((2, 64, 1536), BF),
            pltpu.VMEM((2, 64, 1536), BF),
            pltpu.VMEM((2, 64, 1536), BF),
            pltpu.VMEM((2, 128, 64), BF),
            pltpu.VMEM((2, 1, 3072), F32),
            pltpu.VMEM((ROWS, 128), BF),
            pltpu.VMEM((8, PART, 128), BF),
            pltpu.VMEM((16 * PIECE, 128), F32),
            pltpu.VMEM((16, PIECE, 128), F32),
            pltpu.VMEM((PIECE, 128), F32),
            pltpu.VMEM((16 * PIECE, 128), F32),
            pltpu.VMEM((PART, 128), BF),
            pltpu.VMEM((ROWS, 128), BF),
            dma((7,)),
            dma((4,)),
            dma((4,)),
            dma((4,)),
            dma((4,)),
            dma((4,)),
            dma((4,)),
            dma((4,)),
            dma((4,)),
            dma((4,)),
            dma((4,)),
        ],
        compiler_params=pltpu.CompilerParams(
            collective_id=0, has_side_effects=True, vmem_limit_bytes=56 << 20
        ),
    )(
        *(
            array.reshape(2, 64, 1536)
            for array in (
                spatial_queries,
                spatial_keys,
                spatial_values,
                temporal_queries,
                temporal_keys,
                temporal_values,
            )
        ),
        output_gradient.reshape(128, 3072),
        spatial_projection,
        temporal_projection,
        adapter_down,
        adapter_up,
        spatial_channel_gate.reshape(1, 3072),
        temporal_channel_gate.reshape(1, 3072),
    )
    return (
        *(array.reshape(1, 2, 64, 1536) for array in outs[:6]),
        outs[6],
        outs[7],
        outs[8].reshape(3072),
        outs[9].reshape(3072),
    )


def solution(mesh):
    tokens = P(None, "tm", "space", None)
    return jax.shard_map(
        shards,
        mesh=mesh,
        in_specs=(tokens,) * 7 + (P(),) * 6,
        out_specs=(tokens,) * 6 + (P(),) * 4,
        check_vma=False,
    )
```

```python
import jax
import jax.numpy as jnp
from jax import lax
from jax.experimental import pallas as pl
from jax.experimental.pallas import tpu as pltpu
from jax.sharding import PartitionSpec as P

MESH = pl.DeviceIdType.MESH
BF = jnp.bfloat16
F32 = jnp.float32
SCALE = 128 ** (-0.5)
NN = (((1,), (0,)), ((), ()))
NT = (((1,), (1,)), ((), ()))
TN = (((0,), (0,)), ((), ()))
ROWS = 2688
PART = 336
PIECE = 24


def dot(a, b, dims):
    return lax.dot_general(a, b, dims, preferred_element_type=F32)


def aligned(value, unit):
    return pl.multiple_of(value, unit)


def kernel(
    sq, sk, sv, tq, tk, tv, og_hbm, ws_hbm, wt_hbm, down_hbm, up_hbm, gs_hbm, gt_hbm,
    o_sq, o_sk, o_sv, o_tq, o_tk, o_tv, r4,
    sr, so, prob, dsc, tr, to, tprob, og, ws, wt, down, up, gs, gt, gb, glow, ga_s, ga_t, ah_s, ah_t,
    low, gate_rows, pr, r1, acc, r2, s2, r3, b4,
    load_sem, s_in, s_out, t_in, t_out, s_home, s_back, t_home, t_back, red_in, red_out,
):
    t = lax.axis_index("tm")
    s = lax.axis_index("space")
    chip = s // 2
    core = lax.rem(s, 2)
    z = s // 4
    xh = lax.rem(chip, 2)
    ia = z * 2 + core
    ib = xh * 8 + t

    loads = [
        pltpu.make_async_copy(src, dst, load_sem.at[n])
        for n, (src, dst) in enumerate(
            ((og_hbm, og), (gs_hbm, gs), (gt_hbm, gt), (up_hbm, up), (down_hbm, down), (ws_hbm, ws), (wt_hbm, wt))
        )
    ]
    for load in loads:
        load.start()

    gate = pltpu.get_barrier_semaphore()

    def greet(device):
        pl.semaphore_signal(gate, inc=1, device_id=device, device_id_type=MESH)

    def greet_space(n, carry):
        greet((t, lax.rem(s + n, 16)))
        return carry

    def greet_tm(n, carry):
        other = lax.rem(t + n, 8)
        greet((other, s))
        greet((other, z * 4 + (1 - xh) * 2 + core))
        return carry

    lax.fori_loop(1, 16, greet_space, 0)
    lax.fori_loop(1, 8, greet_tm, 0)
    pl.semaphore_wait(gate, 29)

    def start_local(src, dst, sem):
        pltpu.make_async_copy(src, dst, sem).start()

    def start_remote(src, dst, send, recv, device):
        pltpu.make_async_remote_copy(
            src, dst, send, recv, device_id=device, device_id_type=MESH
        ).start()

    def await_bytes(ref, sem):
        pltpu.make_async_copy(ref, ref, sem).wait()

    WIDTH = (256, 128)

    def spatial_out(src, i):
        def ends(d, k):
            col = aligned(lax.rem(d, 4) * 384 + k * 256, 128)
            return (
                src.at[d // 4, :, pl.ds(col, WIDTH[k])],
                sr.at[i, pl.ds(aligned(s * 64, 64), 64), pl.ds(0, WIDTH[k])],
            )

        def step(n, carry):
            d = lax.rem(chip + n, 8)
            for k in (0, 1):
                a, b = ends(d, k)
                start_remote(a, b, s_out.at[i], s_in.at[i], (t, d * 2 + k))
            return carry

        lax.fori_loop(1, 8, step, 0)
        for k in (0, 1):
            a, b = ends(chip, k)

            @pl.when(core == k)
            def _():
                start_local(a, b, s_in.at[i])

            @pl.when(core != k)
            def _():
                start_remote(a, b, s_out.at[i], s_in.at[i], (t, chip * 2 + k))

    def spatial_arrived(i):
        @pl.when(core == 0)
        def _():
            await_bytes(sr.at[i], s_in.at[i])

        @pl.when(core == 1)
        def _():
            await_bytes(sr.at[i, :, pl.ds(0, 128)], s_in.at[i])

    def spatial_back(j, home):
        for k in (0, 1):

            @pl.when(core == k)
            def _():
                col = aligned(lax.rem(chip, 4) * 384 + k * 256, 128)
                dst = home.at[chip // 4, :, pl.ds(col, WIDTH[k])]

                def src(d):
                    return so.at[j, pl.ds(aligned(d * 64, 64), 64), pl.ds(0, WIDTH[k])]

                def step(n, carry):
                    d = lax.rem(s + n, 16)
                    start_remote(src(d), dst, s_back.at[j], s_home.at[j], (t, d))
                    return carry

                lax.fori_loop(1, 16, step, 0)
                start_local(src(s), dst, s_home.at[j])

    def temporal_out(src, i):
        def ends(d):
            row = aligned(lax.rem(d, 4) * 16, 16)
            col = aligned((d // 4) * 768, 128)
            return src.at[:, pl.ds(row, 16), pl.ds(col, 768)], tr.at[i, pl.ds(2 * t, 2)]

        def step(n, carry):
            d = lax.rem(t + n, 8)
            a, b = ends(d)
            start_remote(a, b, t_out.at[i], t_in.at[i], (d, s))
            return carry

        lax.fori_loop(1, 8, step, 0)
        a, b = ends(t)
        start_local(a, b, t_in.at[i])

    def temporal_back(j, home):
        row = aligned(lax.rem(t, 4) * 16, 16)
        col = aligned((t // 4) * 768, 128)
        dst = home.at[:, pl.ds(row, 16), pl.ds(col, 768)]

        def step(n, carry):
            d = lax.rem(t + n, 8)
            start_remote(to.at[j, pl.ds(2 * d, 2)], dst, t_back.at[j], t_home.at[j], (d, s))
            return carry

        lax.fori_loop(1, 8, step, 0)
        start_local(to.at[j, pl.ds(2 * t, 2)], dst, t_home.at[j])

    for i, src in enumerate((sq, sk, sv)):
        spatial_out(src, i)

    def attention_gradient(b, channel_gate, weight, weight_load, home):
        branch = (og[...].astype(F32) * channel_gate[...]).astype(BF)
        gb[b] = branch
        small = dot(branch, up[...], NT).astype(BF)
        glow[b] = small
        weight_load.wait()

        def step(n, carry):
            rows = pl.ds(aligned(n * 256, 256), 256)
            part = dot(gb[b], weight[rows, :], NT) + dot(small, down[:, rows], NN)
            home[:, :, rows] = part.astype(BF).reshape(2, 64, 256)
            return carry

        lax.fori_loop(0, 6, step, 0)

    for i, src in enumerate((tq, tk, tv)):
        temporal_out(src, i)
    for load in loads[:5]:
        load.wait()
    attention_gradient(0, gs, ws, loads[5], ga_s)
    spatial_out(ga_s, 3)
    attention_gradient(1, gt, wt, loads[6], ga_t)
    temporal_out(ga_t, 3)

    heads = 2 - core
    for i in range(3):
        spatial_arrived(i)

    def spatial_forward(h, carry):
        c = pl.ds(aligned(h * 128, 128), 128)
        keys = sr[1, :, c]
        values = sr[2, :, c]
        for n in range(4):
            r = pl.ds(n * 256, 256)
            scores = dot(sr[0, r, c], keys, NT) * SCALE
            expd = jnp.exp(scores - jnp.max(scores, axis=1, keepdims=True))
            total = jnp.sum(expd, axis=1, keepdims=True)
            low_prob = (expd * (1.0 / total)).astype(BF)
            prob[h, r, :] = low_prob
            so[0, r, c] = dot(low_prob, values, NN).astype(BF)
        return carry

    lax.fori_loop(0, heads, spatial_forward, 0)
    spatial_back(0, ah_s)

    def temporal_load(i, h):
        return tr[i, :, :, pl.ds(h * 128, 128)].reshape(256, 128)

    def temporal_store(j, h, value):
        to[j, :, :, pl.ds(h * 128, 128)] = value.astype(BF).reshape(16, 16, 128)

    for i in range(3):
        await_bytes(tr.at[i], t_in.at[i])
    same_patch = lax.rem(lax.broadcasted_iota(jnp.int32, (256, 256), 0), 16) == lax.rem(
        lax.broadcasted_iota(jnp.int32, (256, 256), 1), 16
    )
    for h in range(6):
        scores = dot(temporal_load(0, h), temporal_load(1, h), NT) * SCALE
        scores = jnp.where(same_patch, scores, -1e30)
        expd = jnp.exp(scores - jnp.max(scores, axis=1, keepdims=True))
        total = jnp.sum(expd, axis=1, keepdims=True)
        low_prob = (expd * (1.0 / total)).astype(BF)
        tprob[h] = low_prob
        temporal_store(0, h, dot(low_prob, temporal_load(2, h), NN))
    temporal_back(0, ah_t)

    spatial_arrived(3)

    def spatial_backward(h, carry):
        c = pl.ds(aligned(h * 128, 128), 128)
        keys = sr[1, :, c]
        values = sr[2, :, c]
        for n in range(4):
            r = pl.ds(n * 256, 256)
            grad = sr[3, r, c]
            row_dot = jnp.sum(
                grad.astype(F32) * so[0, r, c].astype(F32), axis=1, keepdims=True
            )
            grad_prob = dot(grad, values, NT)
            grad_scores = (prob[h, r, :].astype(F32) * (grad_prob - row_dot)).astype(BF)
            dsc[r, :] = grad_scores
            so[1, r, c] = (dot(grad_scores, keys, NN) * SCALE).astype(BF)
        queries_t = sr[0, :, c].T
        grads_t = sr[3, :, c].T
        for n in range(4):
            r = pl.ds(n * 256, 256)
            so[2, r, c] = (dot(queries_t, dsc[:, r], NN) * SCALE).T.astype(BF)
            so[3, r, c] = dot(grads_t, prob[h, :, r], NN).T.astype(BF)
        return carry

    lax.fori_loop(0, heads, spatial_backward, 0)
    for j, home in ((1, o_sq), (2, o_sk), (3, o_sv)):
        spatial_back(j, home)

    await_bytes(tr.at[3], t_in.at[3])
    for h in range(6):
        queries, keys, values, grad = (temporal_load(i, h) for i in range(4))
        attended = to[0, :, :, pl.ds(h * 128, 128)].reshape(256, 128)
        row_dot = jnp.sum(grad.astype(F32) * attended.astype(F32), axis=1, keepdims=True)
        low_prob = tprob[h]
        grad_scores = (low_prob.astype(F32) * (dot(grad, values, NT) - row_dot)).astype(BF)
        temporal_store(1, h, dot(grad_scores, keys, NN) * SCALE)
        temporal_store(2, h, dot(grad_scores, queries, TN) * SCALE)
        temporal_store(3, h, dot(low_prob, grad, TN))
    for j, home in ((1, o_tq), (2, o_tk), (3, o_tv)):
        temporal_back(j, home)

    def adapter(b, home, arrived, weight):
        await_bytes(home, arrived)
        rows = home[...].reshape(128, 1536)
        small = dot(rows, down[...], NT).astype(BF)
        low[b] = small

        def step(n, carry):
            c = pl.ds(aligned(n * 512, 512), 512)
            branch = dot(home[...].reshape(128, 1536), weight[:, c], NN) + dot(low[b], up[:, c], NN)
            gate_rows[b, :, c] = jnp.sum(og[:, c].astype(F32) * branch, axis=0, keepdims=True)
            return carry

        lax.fori_loop(0, 6, step, 0)

    adapter(0, ah_s, s_home.at[0], ws)
    adapter(1, ah_t, t_home.at[0], wt)

    low_st = low[0].astype(F32).T.astype(BF)
    low_tt = low[1].astype(F32).T.astype(BF)
    glow_st = glow[0].astype(F32).T.astype(BF)
    glow_tt = glow[1].astype(F32).T.astype(BF)
    line = lax.broadcasted_iota(jnp.int32, (16, 128), 0)
    for j in range(24):
        c = pl.ds(j * 128, 128)
        pr[pl.ds(j * 80, 64), :] = (
            dot(low_st, gb[0, :, c], NN) + dot(low_tt, gb[1, :, c], NN)
        ).astype(BF)
        pr[pl.ds(j * 80 + 64, 16), :] = jnp.where(
            line == 0, gate_rows[0, :, c], jnp.where(line == 1, gate_rows[1, :, c], 0.0)
        ).astype(BF)
    for j in range(12):
        c = pl.ds(j * 128, 128)
        pr[pl.ds(1920 + j * 64, 64), :] = (
            dot(glow_st, ah_s[:, :, c].reshape(128, 128), NN)
            + dot(glow_tt, ah_t[:, :, c].reshape(128, 128), NN)
        ).astype(BF)

    def in_a(j):
        return (t, (j // 2) * 4 + xh * 2 + lax.rem(j, 2))

    def in_b(j):
        return (lax.rem(j, 8), z * 4 + (j // 8) * 2 + core)

    def exchange(stage, size, mine, device, src, dst):
        def step(n, carry):
            j = lax.rem(mine + n, size)
            start_remote(src(j), dst, red_out.at[stage], red_in.at[stage], device(j))
            return carry

        lax.fori_loop(1, size, step, 0)
        start_local(src(mine), dst, red_in.at[stage])

    exchange(
        0, 8, ia, in_a,
        lambda j: pr.at[pl.ds(aligned(j * PART, 16), PART), :],
        r1.at[ia],
    )
    await_bytes(r1, red_in.at[0])
    total = r1[0].astype(F32)
    for n in range(1, 8):
        total = total + r1[n].astype(F32)
    acc[pl.ds(0, PART), :] = total
    acc[pl.ds(PART, 16 * PIECE - PART), :] = jnp.zeros((16 * PIECE - PART, 128), F32)

    exchange(
        1, 16, ib, in_b,
        lambda j: acc.at[pl.ds(aligned(j * PIECE, 8), PIECE), :],
        r2.at[ib],
    )
    await_bytes(r2, red_in.at[1])
    total = r2[0]
    for n in range(1, 16):
        total = total + r2[n]
    s2[...] = total

    exchange(2, 16, ib, in_b, lambda j: s2, r3.at[pl.ds(aligned(ib * PIECE, 8), PIECE), :])
    await_bytes(r3, red_in.at[2])
    b4[...] = r3[pl.ds(0, PART), :].astype(BF)

    exchange(3, 8, ia, in_a, lambda j: b4, r4.at[pl.ds(aligned(ia * PART, 16), PART), :])
    await_bytes(r4, red_in.at[3])
    for j, (s_ref, t_ref) in enumerate(((None, None), (o_sq, o_tq), (o_sk, o_tk), (o_sv, o_tv))):
        if j > 0:
            await_bytes(s_ref, s_home.at[j])
            await_bytes(t_ref, t_home.at[j])
    for i in range(4):
        await_bytes(tr.at[0, pl.ds(0, 14)], t_out.at[i])
        await_bytes(to.at[0, pl.ds(0, 14)], t_back.at[i])
        for k in (0, 1):

            @pl.when(core == k)
            def _():
                await_bytes(og.at[pl.ds(0, 64), pl.ds(0, 3072 - WIDTH[k])], s_out.at[i])
                await_bytes(so.at[0, pl.ds(0, 960), pl.ds(0, WIDTH[k])], s_back.at[i])

    await_bytes(pr.at[pl.ds(0, 7 * PART), :], red_out.at[0])
    await_bytes(acc.at[pl.ds(0, 15 * PIECE), :], red_out.at[1])
    await_bytes(acc.at[pl.ds(0, 15 * PIECE), :], red_out.at[2])
    await_bytes(pr.at[pl.ds(0, 7 * PART), :], red_out.at[3])


def finish(*refs):
    sources, r4, targets = refs[:6], refs[6], refs[7:13]
    o_down, o_up, o_gs, o_gt, held, sem = refs[13:]
    first = [
        pltpu.make_async_copy(src, held.at[n], sem.at[0, n]) for n, src in enumerate(sources)
    ]
    second = [
        pltpu.make_async_copy(held.at[n], dst, sem.at[1, n]) for n, dst in enumerate(targets)
    ]
    for copy in first:
        copy.start()
    for before, after in zip(first, second, strict=True):
        before.wait()
        after.start()
    for j in range(24):
        c = pl.ds(j * 128, 128)
        o_up[:, c] = r4[pl.ds(j * 80, 64), :].astype(F32)
        tail = r4[pl.ds(j * 80 + 64, 16), :].astype(F32)
        o_gs[:, c] = tail[0:1]
        o_gt[:, c] = tail[1:2]
    for j in range(12):
        o_down[:, pl.ds(j * 128, 128)] = r4[pl.ds(1920 + j * 64, 64), :].astype(F32)

    for copy in second:
        copy.wait()


def shards(
    spatial_queries,
    spatial_keys,
    spatial_values,
    temporal_queries,
    temporal_keys,
    temporal_values,
    output_gradient,
    spatial_projection,
    temporal_projection,
    adapter_down,
    adapter_up,
    spatial_channel_gate,
    temporal_channel_gate,
):
    tokens = jax.ShapeDtypeStruct((2, 64, 1536), BF)
    dma = pltpu.SemaphoreType.DMA
    outs = pl.pallas_call(
        kernel,
        out_shape=(tokens,) * 6
        + (jax.ShapeDtypeStruct((ROWS, 128), BF),),
        in_specs=[pl.BlockSpec(memory_space=pl.ANY)] * 13,
        out_specs=[pl.BlockSpec(memory_space=pl.ANY)] * 6
        + [pl.BlockSpec(memory_space=pltpu.VMEM)],
        scratch_shapes=[
            pltpu.VMEM((4, 1024, 256), BF),
            pltpu.VMEM((4, 1024, 256), BF),
            pltpu.VMEM((2, 1024, 1024), BF),
            pltpu.VMEM((1024, 1024), BF),
            pltpu.VMEM((4, 16, 16, 768), BF),
            pltpu.VMEM((4, 16, 16, 768), BF),
            pltpu.VMEM((6, 256, 256), BF),
            pltpu.VMEM((128, 3072), BF),
            pltpu.VMEM((1536, 3072), BF),
            pltpu.VMEM((1536, 3072), BF),
            pltpu.VMEM((64, 1536), BF),
            pltpu.VMEM((64, 3072), BF),
            pltpu.VMEM((1, 3072), F32),
            pltpu.VMEM((1, 3072), F32),
            pltpu.VMEM((2, 128, 3072), BF),
            pltpu.VMEM((2, 128, 64), BF),
            pltpu.VMEM((2, 64, 1536), BF),
            pltpu.VMEM((2, 64, 1536), BF),
            pltpu.VMEM((2, 64, 1536), BF),
            pltpu.VMEM((2, 64, 1536), BF),
            pltpu.VMEM((2, 128, 64), BF),
            pltpu.VMEM((2, 1, 3072), F32),
            pltpu.VMEM((ROWS, 128), BF),
            pltpu.VMEM((8, PART, 128), BF),
            pltpu.VMEM((16 * PIECE, 128), F32),
            pltpu.VMEM((16, PIECE, 128), F32),
            pltpu.VMEM((PIECE, 128), F32),
            pltpu.VMEM((16 * PIECE, 128), F32),
            pltpu.VMEM((PART, 128), BF),
            dma((7,)),
            dma((4,)),
            dma((4,)),
            dma((4,)),
            dma((4,)),
            dma((4,)),
            dma((4,)),
            dma((4,)),
            dma((4,)),
            dma((4,)),
            dma((4,)),
        ],
        compiler_params=pltpu.CompilerParams(
            collective_id=0, has_side_effects=True, vmem_limit_bytes=56 << 20
        ),
    )(
        *(
            array.reshape(2, 64, 1536)
            for array in (
                spatial_queries,
                spatial_keys,
                spatial_values,
                temporal_queries,
                temporal_keys,
                temporal_values,
            )
        ),
        output_gradient.reshape(128, 3072),
        spatial_projection,
        temporal_projection,
        adapter_down.T,
        adapter_up,
        spatial_channel_gate.reshape(1, 3072),
        temporal_channel_gate.reshape(1, 3072),
    )
    outs = pl.pallas_call(
        finish,
        out_shape=(tokens,) * 6
        + (
            jax.ShapeDtypeStruct((64, 1536), F32),
            jax.ShapeDtypeStruct((64, 3072), F32),
            jax.ShapeDtypeStruct((1, 3072), F32),
            jax.ShapeDtypeStruct((1, 3072), F32),
        ),
        in_specs=[pl.BlockSpec(memory_space=pltpu.HBM)] * 6
        + [pl.BlockSpec(memory_space=pltpu.VMEM)],
        out_specs=[pl.BlockSpec(memory_space=pltpu.HBM)] * 6
        + [pl.BlockSpec(memory_space=pltpu.VMEM)] * 4,
        scratch_shapes=[pltpu.VMEM((6, 2, 64, 1536), BF), dma((2, 6))],
        compiler_params=pltpu.CompilerParams(vmem_limit_bytes=56 << 20),
    )(*outs)
    return (
        *(array.reshape(1, 2, 64, 1536) for array in outs[:6]),
        outs[6].T,
        outs[7],
        outs[8].reshape(3072),
        outs[9].reshape(3072),
    )


def solution(mesh):
    tokens = P(None, "tm", "space", None)
    return jax.shard_map(
        shards,
        mesh=mesh,
        in_specs=(tokens,) * 7 + (P(),) * 6,
        out_specs=(tokens,) * 6 + (P(),) * 4,
        check_vma=False,
    )
```

```python
import jax
import jax.numpy as jnp
from jax import lax
from jax.experimental import pallas as pl
from jax.experimental.pallas import tpu as pltpu
from jax.sharding import PartitionSpec as P

MESH = pl.DeviceIdType.MESH
BF = jnp.bfloat16
F32 = jnp.float32
SCALE = 128 ** (-0.5)
NN = (((1,), (0,)), ((), ()))
NT = (((1,), (1,)), ((), ()))
TN = (((0,), (0,)), ((), ()))
ROWS = 2560
HALF = 1280
PIECE = 80


def dot(a, b, dims):
    return lax.dot_general(a, b, dims, preferred_element_type=F32)


def aligned(value, unit):
    return pl.multiple_of(value, unit)


def kernel(
    sq, sk, sv, tq, tk, tv, og_hbm, ws_hbm, wt_hbm, down_hbm, up_hbm, gs_hbm, gt_hbm,
    o_sq, o_sk, o_sv, o_tq, o_tk, o_tv, r4,
    sr, so, prob, dsc, tr, to, tprob, og, ws, wt, down, up, gs, gt, gb, glow, ga_s, ga_t, ah_s, ah_t,
    low, gate_rows, pr, r_core, half, r_yz, sum_yz, r_x, sum_x, r_all,
    load_sem, s_in, s_out, t_in, t_out, s_home, s_back, t_home, t_back, red_in, red_out,
):
    t = lax.axis_index("tm")
    s = lax.axis_index("space")
    chip = s // 2
    core = lax.rem(s, 2)
    z = s // 4
    xh = lax.rem(chip, 2)
    xl = t // 4
    y = lax.rem(t, 4)
    plane = y * 4 + z

    loads = [
        pltpu.make_async_copy(src, dst, load_sem.at[n])
        for n, (src, dst) in enumerate(
            ((og_hbm, og), (gs_hbm, gs), (gt_hbm, gt), (up_hbm, up), (down_hbm, down), (ws_hbm, ws), (wt_hbm, wt))
        )
    ]
    for load in loads:
        load.start()

    gate = pltpu.get_barrier_semaphore()

    def greet(device):
        pl.semaphore_signal(gate, inc=1, device_id=device, device_id_type=MESH)

    def greet_space(n, carry):
        greet((t, lax.rem(s + n, 16)))
        return carry

    def greet_tm(n, carry):
        greet((lax.rem(t + n, 8), s))
        return carry

    def greet_plane(n, carry):
        other_y = lax.rem(y + 1 + n // 3, 4)
        other_z = lax.rem(z + 1 + lax.rem(n, 3), 4)
        greet((xl * 4 + other_y, other_z * 4 + xh * 2 + core))
        return carry

    lax.fori_loop(1, 16, greet_space, 0)
    lax.fori_loop(1, 8, greet_tm, 0)
    lax.fori_loop(0, 9, greet_plane, 0)
    greet(((1 - xl) * 4 + y, z * 4 + (1 - xh) * 2 + core))
    pl.semaphore_wait(gate, 32)

    def start_local(src, dst, sem):
        pltpu.make_async_copy(src, dst, sem).start()

    def start_remote(src, dst, send, recv, device):
        pltpu.make_async_remote_copy(
            src, dst, send, recv, device_id=device, device_id_type=MESH
        ).start()

    def await_bytes(ref, sem):
        pltpu.make_async_copy(ref, ref, sem).wait()

    WIDTH = (256, 128)

    def spatial_out(src, i):
        def ends(d, k):
            col = aligned(lax.rem(d, 4) * 384 + k * 256, 128)
            return (
                src.at[d // 4, :, pl.ds(col, WIDTH[k])],
                sr.at[i, pl.ds(aligned(s * 64, 64), 64), pl.ds(0, WIDTH[k])],
            )

        def step(n, carry):
            d = lax.rem(chip + n, 8)
            for k in (0, 1):
                a, b = ends(d, k)
                start_remote(a, b, s_out.at[i], s_in.at[i], (t, d * 2 + k))
            return carry

        lax.fori_loop(1, 8, step, 0)
        for k in (0, 1):
            a, b = ends(chip, k)

            @pl.when(core == k)
            def _():
                start_local(a, b, s_in.at[i])

            @pl.when(core != k)
            def _():
                start_remote(a, b, s_out.at[i], s_in.at[i], (t, chip * 2 + k))

    def spatial_arrived(i):
        @pl.when(core == 0)
        def _():
            await_bytes(sr.at[i], s_in.at[i])

        @pl.when(core == 1)
        def _():
            await_bytes(sr.at[i, :, pl.ds(0, 128)], s_in.at[i])

    def spatial_back(j, home):
        for k in (0, 1):

            @pl.when(core == k)
            def _():
                col = aligned(lax.rem(chip, 4) * 384 + k * 256, 128)
                dst = home.at[chip // 4, :, pl.ds(col, WIDTH[k])]

                def src(d):
                    return so.at[j, pl.ds(aligned(d * 64, 64), 64), pl.ds(0, WIDTH[k])]

                def step(n, carry):
                    d = lax.rem(s + n, 16)
                    start_remote(src(d), dst, s_back.at[j], s_home.at[j], (t, d))
                    return carry

                lax.fori_loop(1, 16, step, 0)
                start_local(src(s), dst, s_home.at[j])

    def temporal_out(src, i):
        def ends(d):
            row = aligned(lax.rem(d, 4) * 16, 16)
            col = aligned((d // 4) * 768, 128)
            return src.at[:, pl.ds(row, 16), pl.ds(col, 768)], tr.at[i, pl.ds(2 * t, 2)]

        def step(n, carry):
            d = lax.rem(t + n, 8)
            a, b = ends(d)
            start_remote(a, b, t_out.at[i], t_in.at[i], (d, s))
            return carry

        lax.fori_loop(1, 8, step, 0)
        a, b = ends(t)
        start_local(a, b, t_in.at[i])

    def temporal_back(j, home):
        row = aligned(lax.rem(t, 4) * 16, 16)
        col = aligned((t // 4) * 768, 128)
        dst = home.at[:, pl.ds(row, 16), pl.ds(col, 768)]

        def step(n, carry):
            d = lax.rem(t + n, 8)
            start_remote(to.at[j, pl.ds(2 * d, 2)], dst, t_back.at[j], t_home.at[j], (d, s))
            return carry

        lax.fori_loop(1, 8, step, 0)
        start_local(to.at[j, pl.ds(2 * t, 2)], dst, t_home.at[j])

    for i, src in enumerate((sq, sk, sv)):
        spatial_out(src, i)

    def attention_gradient(b, channel_gate, weight, weight_load, home):
        branch = (og[...].astype(F32) * channel_gate[...]).astype(BF)
        gb[b] = branch
        small = dot(branch, up[...], NT).astype(BF)
        glow[b] = small
        weight_load.wait()

        def step(n, carry):
            rows = pl.ds(aligned(n * 256, 256), 256)
            part = dot(gb[b], weight[rows, :], NT) + dot(small, down[:, rows], NN)
            home[:, :, rows] = part.astype(BF).reshape(2, 64, 256)
            return carry

        lax.fori_loop(0, 6, step, 0)

    for i, src in enumerate((tq, tk, tv)):
        temporal_out(src, i)
    for load in loads[:5]:
        load.wait()
    attention_gradient(0, gs, ws, loads[5], ga_s)
    attention_gradient(1, gt, wt, loads[6], ga_t)

    heads = 2 - core
    for i in range(3):
        spatial_arrived(i)

    def spatial_forward(h, carry):
        c = pl.ds(aligned(h * 128, 128), 128)
        keys = sr[1, :, c]
        values = sr[2, :, c]
        for n in range(4):
            r = pl.ds(n * 256, 256)
            scores = dot(sr[0, r, c], keys, NT) * SCALE
            expd = jnp.exp(scores - jnp.max(scores, axis=1, keepdims=True))
            total = jnp.sum(expd, axis=1, keepdims=True)
            low_prob = (expd * (1.0 / total)).astype(BF)
            prob[h, r, :] = low_prob
            so[0, r, c] = dot(low_prob, values, NN).astype(BF)
        return carry

    lax.fori_loop(0, heads, spatial_forward, 0)
    spatial_back(0, ah_s)

    def temporal_load(i, h):
        return tr[i, :, :, pl.ds(h * 128, 128)].reshape(256, 128)

    def temporal_store(j, h, value):
        to[j, :, :, pl.ds(h * 128, 128)] = value.astype(BF).reshape(16, 16, 128)

    for i in range(3):
        await_bytes(tr.at[i], t_in.at[i])
    same_patch = lax.rem(lax.broadcasted_iota(jnp.int32, (256, 256), 0), 16) == lax.rem(
        lax.broadcasted_iota(jnp.int32, (256, 256), 1), 16
    )
    for h in range(6):
        scores = dot(temporal_load(0, h), temporal_load(1, h), NT) * SCALE
        scores = jnp.where(same_patch, scores, -1e30)
        expd = jnp.exp(scores - jnp.max(scores, axis=1, keepdims=True))
        total = jnp.sum(expd, axis=1, keepdims=True)
        low_prob = (expd * (1.0 / total)).astype(BF)
        tprob[h] = low_prob
        temporal_store(0, h, dot(low_prob, temporal_load(2, h), NN))
    temporal_back(0, ah_t)

    spatial_out(ga_s, 3)
    temporal_out(ga_t, 3)

    def adapter(b, home, arrived, weight):
        await_bytes(home, arrived)
        rows = home[...].reshape(128, 1536)
        small = dot(rows, down[...], NT).astype(BF)
        low[b] = small

        for n in range(6):
            c = pl.ds(n * 512, 512)
            branch = dot(rows, weight[:, c], NN) + dot(small, up[:, c], NN)
            sums = jnp.sum(og[:, c].astype(F32) * branch, axis=0, keepdims=True)
            for m in range(4):
                gate_rows[pl.ds(b * 24 + n * 4 + m, 1), :] = sums[:, m * 128 : (m + 1) * 128]

    adapter(0, ah_s, s_home.at[0], ws)
    adapter(1, ah_t, t_home.at[0], wt)

    low_st = low[0].astype(F32).T.astype(BF)
    low_tt = low[1].astype(F32).T.astype(BF)
    glow_st = glow[0].astype(F32).T.astype(BF)
    glow_tt = glow[1].astype(F32).T.astype(BF)
    for j in range(24):
        c = pl.ds(j * 128, 128)
        pr[pl.ds(j * 64, 64), :] = (
            dot(low_st, gb[0, :, c], NN) + dot(low_tt, gb[1, :, c], NN)
        ).astype(BF)
    for j in range(12):
        c = pl.ds(j * 128, 128)
        pr[pl.ds(1536 + j * 64, 64), :] = (
            dot(glow_st, ah_s[:, :, c].reshape(128, 128), NN)
            + dot(glow_tt, ah_t[:, :, c].reshape(128, 128), NN)
        ).astype(BF)
    pr[pl.ds(2304, 48), :] = gate_rows[...].astype(BF)
    pr[pl.ds(2352, ROWS - 2352), :] = jnp.zeros((ROWS - 2352, 128), BF)

    other_core = (t, s + 1 - 2 * core)

    def in_plane(j):
        return (xl * 4 + j // 4, lax.rem(j, 4) * 4 + xh * 2 + core)

    def to_plane(stage, src, dst):
        def step(n, carry):
            j = lax.rem(plane + n, 16)
            start_remote(src(j), dst, red_out.at[stage], red_in.at[stage], in_plane(j))
            return carry

        lax.fori_loop(1, 16, step, 0)
        start_local(src(plane), dst, red_in.at[stage])

    start_remote(
        pr.at[pl.ds(aligned((1 - core) * HALF, 16), HALF), :],
        r_core,
        red_out.at[0],
        red_in.at[0],
        other_core,
    )

    await_bytes(r_core, red_in.at[0])
    mine = pr[pl.ds(aligned(core * HALF, 16), HALF), :].astype(F32)
    half[...] = (mine + r_core[...].astype(F32)).astype(BF)
    to_plane(1, lambda j: half.at[pl.ds(aligned(j * PIECE, 16), PIECE), :], r_yz.at[plane])

    spatial_arrived(3)

    def spatial_backward(h, carry):
        c = pl.ds(aligned(h * 128, 128), 128)
        keys = sr[1, :, c]
        values = sr[2, :, c]
        for n in range(4):
            r = pl.ds(n * 256, 256)
            grad = sr[3, r, c]
            row_dot = jnp.sum(
                grad.astype(F32) * so[0, r, c].astype(F32), axis=1, keepdims=True
            )
            grad_prob = dot(grad, values, NT)
            grad_scores = (prob[h, r, :].astype(F32) * (grad_prob - row_dot)).astype(BF)
            dsc[r, :] = grad_scores
            so[1, r, c] = (dot(grad_scores, keys, NN) * SCALE).astype(BF)
        queries_t = sr[0, :, c].T
        grads_t = sr[3, :, c].T
        for n in range(4):
            r = pl.ds(n * 256, 256)
            so[2, r, c] = (dot(queries_t, dsc[:, r], NN) * SCALE).T.astype(BF)
            so[3, r, c] = dot(grads_t, prob[h, :, r], NN).T.astype(BF)
        return carry

    lax.fori_loop(0, heads, spatial_backward, 0)

    spatial_back(1, o_sq)
    await_bytes(tr.at[3], t_in.at[3])
    for h in range(6):
        queries, keys, values, grad = (temporal_load(i, h) for i in range(4))
        attended = to[0, :, :, pl.ds(h * 128, 128)].reshape(256, 128)
        row_dot = jnp.sum(grad.astype(F32) * attended.astype(F32), axis=1, keepdims=True)
        low_prob = tprob[h]
        grad_scores = (low_prob.astype(F32) * (dot(grad, values, NT) - row_dot)).astype(BF)
        temporal_store(1, h, dot(grad_scores, keys, NN) * SCALE)
        temporal_store(2, h, dot(grad_scores, queries, TN) * SCALE)
        temporal_store(3, h, dot(low_prob, grad, TN))

    temporal_back(1, o_tq)
    await_bytes(r_yz, red_in.at[1])
    total = r_yz[0].astype(F32)
    for n in range(1, 16):
        total = total + r_yz[n].astype(F32)
    sum_yz[...] = total.astype(BF)
    slot = r_x.at[xl * 2 + xh]
    for flip_l, flip_h in ((0, 1), (1, 0), (1, 1)):
        device_l = 1 - xl if flip_l else xl
        device_h = 1 - xh if flip_h else xh
        start_remote(
            sum_yz,
            slot,
            red_out.at[2],
            red_in.at[2],
            (device_l * 4 + y, z * 4 + device_h * 2 + core),
        )
    start_local(sum_yz, slot, red_in.at[2])

    spatial_back(2, o_sk)
    spatial_back(3, o_sv)
    temporal_back(2, o_tk)
    temporal_back(3, o_tv)
    await_bytes(r_x, red_in.at[2])
    total = r_x[0].astype(F32)
    for n in range(1, 4):
        total = total + r_x[n].astype(F32)
    sum_x[...] = total.astype(BF)
    to_plane(3, lambda j: sum_x, r_all.at[pl.ds(aligned(plane * PIECE, 16), PIECE), :])
    await_bytes(r_all, red_in.at[3])
    rows = r4.at[pl.ds(aligned(core * HALF, 16), HALF), :]
    start_remote(r_all, rows, red_out.at[4], red_in.at[4], other_core)
    start_local(r_all, rows, red_in.at[4])
    await_bytes(r4, red_in.at[4])

    for j, (s_ref, t_ref) in enumerate(((None, None), (o_sq, o_tq), (o_sk, o_tk), (o_sv, o_tv))):
        if j > 0:
            await_bytes(s_ref, s_home.at[j])
            await_bytes(t_ref, t_home.at[j])
    for i in range(4):
        await_bytes(tr.at[0, pl.ds(0, 14)], t_out.at[i])
        await_bytes(to.at[0, pl.ds(0, 14)], t_back.at[i])
        for k in (0, 1):

            @pl.when(core == k)
            def _():
                await_bytes(og.at[pl.ds(0, 64), pl.ds(0, 3072 - WIDTH[k])], s_out.at[i])
                await_bytes(so.at[0, pl.ds(0, 960), pl.ds(0, WIDTH[k])], s_back.at[i])

    for stage, rows in enumerate((HALF, 15 * PIECE, 3 * PIECE, 15 * PIECE, HALF)):
        await_bytes(pr.at[pl.ds(0, rows), :], red_out.at[stage])


def finish(*refs):
    sources, r4, targets = refs[:6], refs[6], refs[7:13]
    o_down, o_up, o_gs, o_gt, held, sem = refs[13:]
    first = [
        pltpu.make_async_copy(src, held.at[n], sem.at[0, n]) for n, src in enumerate(sources)
    ]
    second = [
        pltpu.make_async_copy(held.at[n], dst, sem.at[1, n]) for n, dst in enumerate(targets)
    ]
    for copy in first:
        copy.start()
    for before, after in zip(first, second, strict=True):
        before.wait()
        after.start()
    gates = r4[pl.ds(2304, 48), :].astype(F32)
    for j in range(24):
        c = pl.ds(j * 128, 128)
        o_up[:, c] = r4[pl.ds(j * 64, 64), :].astype(F32)
        o_gs[:, c] = gates[j : j + 1]
        o_gt[:, c] = gates[24 + j : 25 + j]
    for j in range(12):
        o_down[:, pl.ds(j * 128, 128)] = r4[pl.ds(1536 + j * 64, 64), :].astype(F32)

    for copy in second:
        copy.wait()


def shards(
    spatial_queries,
    spatial_keys,
    spatial_values,
    temporal_queries,
    temporal_keys,
    temporal_values,
    output_gradient,
    spatial_projection,
    temporal_projection,
    adapter_down,
    adapter_up,
    spatial_channel_gate,
    temporal_channel_gate,
):
    tokens = jax.ShapeDtypeStruct((2, 64, 1536), BF)
    dma = pltpu.SemaphoreType.DMA
    outs = pl.pallas_call(
        kernel,
        out_shape=(tokens,) * 6
        + (jax.ShapeDtypeStruct((ROWS, 128), BF),),
        in_specs=[pl.BlockSpec(memory_space=pl.ANY)] * 13,
        out_specs=[pl.BlockSpec(memory_space=pl.ANY)] * 6
        + [pl.BlockSpec(memory_space=pltpu.VMEM)],
        scratch_shapes=[
            pltpu.VMEM((4, 1024, 256), BF),
            pltpu.VMEM((4, 1024, 256), BF),
            pltpu.VMEM((2, 1024, 1024), BF),
            pltpu.VMEM((1024, 1024), BF),
            pltpu.VMEM((4, 16, 16, 768), BF),
            pltpu.VMEM((4, 16, 16, 768), BF),
            pltpu.VMEM((6, 256, 256), BF),
            pltpu.VMEM((128, 3072), BF),
            pltpu.VMEM((1536, 3072), BF),
            pltpu.VMEM((1536, 3072), BF),
            pltpu.VMEM((64, 1536), BF),
            pltpu.VMEM((64, 3072), BF),
            pltpu.VMEM((1, 3072), F32),
            pltpu.VMEM((1, 3072), F32),
            pltpu.VMEM((2, 128, 3072), BF),
            pltpu.VMEM((2, 128, 64), BF),
            pltpu.VMEM((2, 64, 1536), BF),
            pltpu.VMEM((2, 64, 1536), BF),
            pltpu.VMEM((2, 64, 1536), BF),
            pltpu.VMEM((2, 64, 1536), BF),
            pltpu.VMEM((2, 128, 64), BF),
            pltpu.VMEM((48, 128), F32),
            pltpu.VMEM((ROWS, 128), BF),
            pltpu.VMEM((HALF, 128), BF),
            pltpu.VMEM((HALF, 128), BF),
            pltpu.VMEM((16, PIECE, 128), BF),
            pltpu.VMEM((PIECE, 128), BF),
            pltpu.VMEM((4, PIECE, 128), BF),
            pltpu.VMEM((PIECE, 128), BF),
            pltpu.VMEM((HALF, 128), BF),
            dma((7,)),
            dma((4,)),
            dma((4,)),
            dma((4,)),
            dma((4,)),
            dma((4,)),
            dma((4,)),
            dma((4,)),
            dma((4,)),
            dma((5,)),
            dma((5,)),
        ],
        compiler_params=pltpu.CompilerParams(
            collective_id=0, has_side_effects=True, vmem_limit_bytes=56 << 20
        ),
    )(
        *(
            array.reshape(2, 64, 1536)
            for array in (
                spatial_queries,
                spatial_keys,
                spatial_values,
                temporal_queries,
                temporal_keys,
                temporal_values,
            )
        ),
        output_gradient.reshape(128, 3072),
        spatial_projection,
        temporal_projection,
        adapter_down.T,
        adapter_up,
        spatial_channel_gate.reshape(1, 3072),
        temporal_channel_gate.reshape(1, 3072),
    )
    outs = pl.pallas_call(
        finish,
        out_shape=(tokens,) * 6
        + (
            jax.ShapeDtypeStruct((64, 1536), F32),
            jax.ShapeDtypeStruct((64, 3072), F32),
            jax.ShapeDtypeStruct((1, 3072), F32),
            jax.ShapeDtypeStruct((1, 3072), F32),
        ),
        in_specs=[pl.BlockSpec(memory_space=pltpu.HBM)] * 6
        + [pl.BlockSpec(memory_space=pltpu.VMEM)],
        out_specs=[pl.BlockSpec(memory_space=pltpu.HBM)] * 6
        + [pl.BlockSpec(memory_space=pltpu.VMEM)] * 4,
        scratch_shapes=[pltpu.VMEM((6, 2, 64, 1536), BF), dma((2, 6))],
        compiler_params=pltpu.CompilerParams(vmem_limit_bytes=56 << 20),
    )(*outs)
    return (
        *(array.reshape(1, 2, 64, 1536) for array in outs[:6]),
        outs[6].T,
        outs[7],
        outs[8].reshape(3072),
        outs[9].reshape(3072),
    )


def solution(mesh):
    tokens = P(None, "tm", "space", None)
    return jax.shard_map(
        shards,
        mesh=mesh,
        in_specs=(tokens,) * 7 + (P(),) * 6,
        out_specs=(tokens,) * 6 + (P(),) * 4,
        check_vma=False,
    )
```

```python
import jax
import jax.numpy as jnp
from jax import lax
from jax.experimental import pallas as pl
from jax.experimental.pallas import tpu as pltpu
from jax.sharding import PartitionSpec as P

MESH = pl.DeviceIdType.MESH
BF = jnp.bfloat16
F32 = jnp.float32
SCALE = 128 ** (-0.5)
NN = (((1,), (0,)), ((), ()))
NT = (((1,), (1,)), ((), ()))
TN = (((0,), (0,)), ((), ()))
ROWS = 2560
HALF = 1280
PIECE = 80


def dot(a, b, dims):
    return lax.dot_general(a, b, dims, preferred_element_type=F32)


def aligned(value, unit):
    return pl.multiple_of(value, unit)


def kernel(
    sq, sk, sv, tq, tk, tv, og_hbm, ws_hbm, wt_hbm, down_hbm, up_hbm, gs_hbm, gt_hbm,
    o_sq, o_sk, o_sv, o_tq, o_tk, o_tv, r4,
    sr, so, prob, dsc, tr, to, tprob, og, ws, wt, down, up, gs, gt, gb, glow, ga_s, ga_t, ah_s, ah_t,
    low, gate_rows, pr, r_core, half, r_yz, sum_yz, r_x, sum_x, r_all,
    load_sem, s_in, s_out, t_in, t_out, s_home, s_back, t_home, t_back, red_in, red_out,
):
    t = lax.axis_index("tm")
    s = lax.axis_index("space")
    chip = s // 2
    core = lax.rem(s, 2)
    z = s // 4
    xh = lax.rem(chip, 2)
    xl = t // 4
    y = lax.rem(t, 4)
    plane = y * 4 + z

    loads = [
        pltpu.make_async_copy(src, dst, load_sem.at[n])
        for n, (src, dst) in enumerate(
            ((og_hbm, og), (gs_hbm, gs), (gt_hbm, gt), (up_hbm, up), (down_hbm, down), (ws_hbm, ws), (wt_hbm, wt))
        )
    ]
    for load in loads:
        load.start()

    gate = pltpu.get_barrier_semaphore()

    def greet(device):
        pl.semaphore_signal(gate, inc=1, device_id=device, device_id_type=MESH)

    def greet_space(n, carry):
        greet((t, lax.rem(s + n, 16)))
        return carry

    def greet_tm(n, carry):
        greet((lax.rem(t + n, 8), s))
        return carry

    def greet_plane(n, carry):
        other_y = lax.rem(y + 1 + n // 3, 4)
        other_z = lax.rem(z + 1 + lax.rem(n, 3), 4)
        greet((xl * 4 + other_y, other_z * 4 + xh * 2 + core))
        return carry

    lax.fori_loop(1, 16, greet_space, 0)
    lax.fori_loop(1, 8, greet_tm, 0)
    lax.fori_loop(0, 9, greet_plane, 0)
    greet(((1 - xl) * 4 + y, z * 4 + (1 - xh) * 2 + core))
    pl.semaphore_wait(gate, 32)

    def start_local(src, dst, sem):
        pltpu.make_async_copy(src, dst, sem).start()

    def start_remote(src, dst, send, recv, device):
        pltpu.make_async_remote_copy(
            src, dst, send, recv, device_id=device, device_id_type=MESH
        ).start()

    def await_bytes(ref, sem):
        pltpu.make_async_copy(ref, ref, sem).wait()

    WIDTH = (256, 128)

    def spatial_out(src, i):
        def ends(d, k):
            col = aligned(lax.rem(d, 4) * 384 + k * 256, 128)
            return (
                src.at[d // 4, :, pl.ds(col, WIDTH[k])],
                sr.at[i, pl.ds(aligned(s * 64, 64), 64), pl.ds(0, WIDTH[k])],
            )

        def step(n, carry):
            d = lax.rem(chip + n, 8)
            for k in (0, 1):
                a, b = ends(d, k)
                start_remote(a, b, s_out.at[i], s_in.at[i], (t, d * 2 + k))
            return carry

        lax.fori_loop(1, 8, step, 0)
        for k in (0, 1):
            a, b = ends(chip, k)

            @pl.when(core == k)
            def _():
                start_local(a, b, s_in.at[i])

            @pl.when(core != k)
            def _():
                start_remote(a, b, s_out.at[i], s_in.at[i], (t, chip * 2 + k))

    def spatial_arrived(i):
        @pl.when(core == 0)
        def _():
            await_bytes(sr.at[i], s_in.at[i])

        @pl.when(core == 1)
        def _():
            await_bytes(sr.at[i, :, pl.ds(0, 128)], s_in.at[i])

    def spatial_back(j, home):
        for k in (0, 1):

            @pl.when(core == k)
            def _():
                col = aligned(lax.rem(chip, 4) * 384 + k * 256, 128)
                dst = home.at[chip // 4, :, pl.ds(col, WIDTH[k])]

                def src(d):
                    return so.at[j, pl.ds(aligned(d * 64, 64), 64), pl.ds(0, WIDTH[k])]

                def step(n, carry):
                    d = lax.rem(s + n, 16)
                    start_remote(src(d), dst, s_back.at[j], s_home.at[j], (t, d))
                    return carry

                lax.fori_loop(1, 16, step, 0)
                start_local(src(s), dst, s_home.at[j])

    def temporal_out(src, i):
        def ends(d):
            row = aligned(lax.rem(d, 4) * 16, 16)
            col = aligned((d // 4) * 768, 128)
            return src.at[:, pl.ds(row, 16), pl.ds(col, 768)], tr.at[i, pl.ds(2 * t, 2)]

        def step(n, carry):
            d = lax.rem(t + n, 8)
            a, b = ends(d)
            start_remote(a, b, t_out.at[i], t_in.at[i], (d, s))
            return carry

        lax.fori_loop(1, 8, step, 0)
        a, b = ends(t)
        start_local(a, b, t_in.at[i])

    def temporal_back(j, home):
        row = aligned(lax.rem(t, 4) * 16, 16)
        col = aligned((t // 4) * 768, 128)
        dst = home.at[:, pl.ds(row, 16), pl.ds(col, 768)]

        def step(n, carry):
            d = lax.rem(t + n, 8)
            start_remote(to.at[j, pl.ds(2 * d, 2)], dst, t_back.at[j], t_home.at[j], (d, s))
            return carry

        lax.fori_loop(1, 8, step, 0)
        start_local(to.at[j, pl.ds(2 * t, 2)], dst, t_home.at[j])

    for i, src in enumerate((sq, sk, sv)):
        spatial_out(src, i)

    def attention_gradient(b, channel_gate, weight, weight_load, home):
        branch = (og[...].astype(F32) * channel_gate[...]).astype(BF)
        gb[b] = branch
        small = dot(branch, up[...], NT).astype(BF)
        glow[b] = small
        weight_load.wait()

        def step(n, carry):
            rows = pl.ds(aligned(n * 256, 256), 256)
            part = dot(gb[b], weight[rows, :], NT) + dot(small, down[:, rows], NN)
            home[:, :, rows] = part.astype(BF).reshape(2, 64, 256)
            return carry

        lax.fori_loop(0, 6, step, 0)

    for i, src in enumerate((tq, tk, tv)):
        temporal_out(src, i)
    for load in loads[:5]:
        load.wait()
    attention_gradient(0, gs, ws, loads[5], ga_s)
    attention_gradient(1, gt, wt, loads[6], ga_t)

    heads = 2 - core
    for i in range(3):
        spatial_arrived(i)

    def spatial_forward(h, carry):
        c = pl.ds(aligned(h * 128, 128), 128)
        keys = sr[1, :, c]
        values = sr[2, :, c]
        for n in range(4):
            r = pl.ds(n * 256, 256)
            scores = dot(sr[0, r, c], keys, NT) * SCALE
            expd = jnp.exp(scores - jnp.max(scores, axis=1, keepdims=True))
            total = jnp.sum(expd, axis=1, keepdims=True)
            low_prob = (expd * (1.0 / total)).astype(BF)
            prob[h, r, :] = low_prob
            so[0, r, c] = dot(low_prob, values, NN).astype(BF)
        return carry

    lax.fori_loop(0, heads, spatial_forward, 0)
    spatial_back(0, ah_s)

    def temporal_load(i, h):
        return tr[i, :, :, pl.ds(h * 128, 128)].reshape(256, 128)

    def temporal_store(j, h, value):
        to[j, :, :, pl.ds(h * 128, 128)] = value.astype(BF).reshape(16, 16, 128)

    for i in range(3):
        await_bytes(tr.at[i], t_in.at[i])
    same_patch = lax.rem(lax.broadcasted_iota(jnp.int32, (256, 256), 0), 16) == lax.rem(
        lax.broadcasted_iota(jnp.int32, (256, 256), 1), 16
    )
    for h in range(6):
        scores = dot(temporal_load(0, h), temporal_load(1, h), NT) * SCALE
        scores = jnp.where(same_patch, scores, -1e30)
        expd = jnp.exp(scores - jnp.max(scores, axis=1, keepdims=True))
        total = jnp.sum(expd, axis=1, keepdims=True)
        low_prob = (expd * (1.0 / total)).astype(BF)
        tprob[h] = low_prob
        temporal_store(0, h, dot(low_prob, temporal_load(2, h), NN))
    temporal_back(0, ah_t)

    spatial_out(ga_s, 3)
    temporal_out(ga_t, 3)

    def adapter(b, home, arrived, weight):
        await_bytes(home, arrived)
        rows = home[...].reshape(128, 1536)
        small = dot(rows, down[...], NT).astype(BF)
        low[b] = small

        for n in range(6):
            c = pl.ds(n * 512, 512)
            branch = dot(rows, weight[:, c], NN) + dot(small, up[:, c], NN)
            sums = jnp.sum(og[:, c].astype(F32) * branch, axis=0, keepdims=True)
            for m in range(4):
                gate_rows[pl.ds(b * 24 + n * 4 + m, 1), :] = sums[:, m * 128 : (m + 1) * 128]

    adapter(0, ah_s, s_home.at[0], ws)
    adapter(1, ah_t, t_home.at[0], wt)

    low_st = low[0].astype(F32).T.astype(BF)
    low_tt = low[1].astype(F32).T.astype(BF)
    glow_st = glow[0].astype(F32).T.astype(BF)
    glow_tt = glow[1].astype(F32).T.astype(BF)
    for j in range(24):
        c = pl.ds(j * 128, 128)
        pr[pl.ds(j * 64, 64), :] = (
            dot(low_st, gb[0, :, c], NN) + dot(low_tt, gb[1, :, c], NN)
        ).astype(BF)
    for j in range(12):
        c = pl.ds(j * 128, 128)
        pr[pl.ds(1536 + j * 64, 64), :] = (
            dot(glow_st, ah_s[:, :, c].reshape(128, 128), NN)
            + dot(glow_tt, ah_t[:, :, c].reshape(128, 128), NN)
        ).astype(BF)
    pr[pl.ds(2304, 48), :] = gate_rows[...].astype(BF)
    pr[pl.ds(2352, ROWS - 2352), :] = jnp.zeros((ROWS - 2352, 128), BF)

    other_core = (t, s + 1 - 2 * core)

    def in_plane(j):
        return (xl * 4 + j // 4, lax.rem(j, 4) * 4 + xh * 2 + core)

    def to_plane(stage, src, dst):
        def step(n, carry):
            j = lax.rem(plane + n, 16)
            start_remote(src(j), dst, red_out.at[stage], red_in.at[stage], in_plane(j))
            return carry

        lax.fori_loop(1, 16, step, 0)
        start_local(src(plane), dst, red_in.at[stage])

    start_remote(
        pr.at[pl.ds(aligned((1 - core) * HALF, 16), HALF), :],
        r_core,
        red_out.at[0],
        red_in.at[0],
        other_core,
    )

    await_bytes(r_core, red_in.at[0])
    mine = pr[pl.ds(aligned(core * HALF, 16), HALF), :].astype(F32)
    half[...] = (mine + r_core[...].astype(F32)).astype(BF)
    to_plane(1, lambda j: half.at[pl.ds(aligned(j * PIECE, 16), PIECE), :], r_yz.at[plane])

    spatial_arrived(3)

    def spatial_backward(h, carry):
        c = pl.ds(aligned(h * 128, 128), 128)
        keys = sr[1, :, c]
        values = sr[2, :, c]
        for n in range(4):
            r = pl.ds(n * 256, 256)
            grad = sr[3, r, c]
            row_dot = jnp.sum(
                grad.astype(F32) * so[0, r, c].astype(F32), axis=1, keepdims=True
            )
            grad_prob = dot(grad, values, NT)
            grad_scores = (prob[h, r, :].astype(F32) * (grad_prob - row_dot)).astype(BF)
            dsc[r, :] = grad_scores
            so[1, r, c] = (dot(grad_scores, keys, NN) * SCALE).astype(BF)
        queries_t = sr[0, :, c].T
        grads_t = sr[3, :, c].T
        for n in range(4):
            r = pl.ds(n * 256, 256)
            so[2, r, c] = (dot(queries_t, dsc[:, r], NN) * SCALE).T.astype(BF)
            so[3, r, c] = dot(grads_t, prob[h, :, r], NN).T.astype(BF)
        return carry

    lax.fori_loop(0, heads, spatial_backward, 0)

    spatial_back(1, o_sq)
    await_bytes(tr.at[3], t_in.at[3])
    for h in range(6):
        queries, keys, values, grad = (temporal_load(i, h) for i in range(4))
        attended = to[0, :, :, pl.ds(h * 128, 128)].reshape(256, 128)
        row_dot = jnp.sum(grad.astype(F32) * attended.astype(F32), axis=1, keepdims=True)
        low_prob = tprob[h]
        grad_scores = (low_prob.astype(F32) * (dot(grad, values, NT) - row_dot)).astype(BF)
        temporal_store(1, h, dot(grad_scores, keys, NN) * SCALE)
        temporal_store(2, h, dot(grad_scores, queries, TN) * SCALE)
        temporal_store(3, h, dot(low_prob, grad, TN))

    temporal_back(1, o_tq)
    await_bytes(r_yz, red_in.at[1])
    total = r_yz[0].astype(F32)
    for n in range(1, 16):
        total = total + r_yz[n].astype(F32)
    sum_yz[...] = total.astype(BF)
    slot = r_x.at[xl * 2 + xh]
    for flip_l, flip_h in ((0, 1), (1, 0), (1, 1)):
        device_l = 1 - xl if flip_l else xl
        device_h = 1 - xh if flip_h else xh
        start_remote(
            sum_yz,
            slot,
            red_out.at[2],
            red_in.at[2],
            (device_l * 4 + y, z * 4 + device_h * 2 + core),
        )
    start_local(sum_yz, slot, red_in.at[2])

    spatial_back(2, o_sk)
    spatial_back(3, o_sv)
    temporal_back(2, o_tk)
    temporal_back(3, o_tv)
    await_bytes(r_x, red_in.at[2])
    total = r_x[0].astype(F32)
    for n in range(1, 4):
        total = total + r_x[n].astype(F32)
    sum_x[...] = total.astype(BF)
    to_plane(3, lambda j: sum_x, r_all.at[pl.ds(aligned(plane * PIECE, 16), PIECE), :])
    await_bytes(r_all, red_in.at[3])
    rows = r4.at[pl.ds(aligned(core * HALF, 16), HALF), :]
    start_remote(r_all, rows, red_out.at[4], red_in.at[4], other_core)
    start_local(r_all, rows, red_in.at[4])
    await_bytes(r4, red_in.at[4])

    for j, (s_ref, t_ref) in enumerate(((None, None), (o_sq, o_tq), (o_sk, o_tk), (o_sv, o_tv))):
        if j > 0:
            await_bytes(s_ref, s_home.at[j])
            await_bytes(t_ref, t_home.at[j])
    for i in range(4):
        await_bytes(tr.at[0, pl.ds(0, 14)], t_out.at[i])
        await_bytes(to.at[0, pl.ds(0, 14)], t_back.at[i])
        for k in (0, 1):

            @pl.when(core == k)
            def _():
                await_bytes(og.at[pl.ds(0, 64), pl.ds(0, 3072 - WIDTH[k])], s_out.at[i])
                await_bytes(so.at[0, pl.ds(0, 960), pl.ds(0, WIDTH[k])], s_back.at[i])

    for stage, rows in enumerate((HALF, 15 * PIECE, 3 * PIECE, 15 * PIECE, HALF)):
        await_bytes(pr.at[pl.ds(0, rows), :], red_out.at[stage])


def finish(*refs):
    sources, r4, targets = refs[:6], refs[6], refs[7:13]
    o_down, o_up, o_gs, o_gt, sem = refs[13:]
    copies = [
        pltpu.make_async_copy(src, dst, sem.at[n])
        for n, (src, dst) in enumerate(zip(sources, targets, strict=True))
    ]
    for copy in copies:
        copy.start()
    gates = r4[pl.ds(2304, 48), :].astype(F32)
    for j in range(24):
        c = pl.ds(j * 128, 128)
        o_up[:, c] = r4[pl.ds(j * 64, 64), :].astype(F32)
        o_gs[:, c] = gates[j : j + 1]
        o_gt[:, c] = gates[24 + j : 25 + j]
    for j in range(12):
        o_down[:, pl.ds(j * 128, 128)] = r4[pl.ds(1536 + j * 64, 64), :].astype(F32)

    for copy in copies:
        copy.wait()


def shards(
    spatial_queries,
    spatial_keys,
    spatial_values,
    temporal_queries,
    temporal_keys,
    temporal_values,
    output_gradient,
    spatial_projection,
    temporal_projection,
    adapter_down,
    adapter_up,
    spatial_channel_gate,
    temporal_channel_gate,
):
    tokens = jax.ShapeDtypeStruct((2, 64, 1536), BF)
    dma = pltpu.SemaphoreType.DMA
    outs = pl.pallas_call(
        kernel,
        out_shape=(pltpu.VMEM((2, 64, 1536), BF),) * 6 + (pltpu.VMEM((ROWS, 128), BF),),
        in_specs=[pl.BlockSpec(memory_space=pl.ANY)] * 13,
        out_specs=[pl.BlockSpec(memory_space=pl.ANY)] * 7,
        scratch_shapes=[
            pltpu.VMEM((4, 1024, 256), BF),
            pltpu.VMEM((4, 1024, 256), BF),
            pltpu.VMEM((2, 1024, 1024), BF),
            pltpu.VMEM((1024, 1024), BF),
            pltpu.VMEM((4, 16, 16, 768), BF),
            pltpu.VMEM((4, 16, 16, 768), BF),
            pltpu.VMEM((6, 256, 256), BF),
            pltpu.VMEM((128, 3072), BF),
            pltpu.VMEM((1536, 3072), BF),
            pltpu.VMEM((1536, 3072), BF),
            pltpu.VMEM((64, 1536), BF),
            pltpu.VMEM((64, 3072), BF),
            pltpu.VMEM((1, 3072), F32),
            pltpu.VMEM((1, 3072), F32),
            pltpu.VMEM((2, 128, 3072), BF),
            pltpu.VMEM((2, 128, 64), BF),
            pltpu.VMEM((2, 64, 1536), BF),
            pltpu.VMEM((2, 64, 1536), BF),
            pltpu.VMEM((2, 64, 1536), BF),
            pltpu.VMEM((2, 64, 1536), BF),
            pltpu.VMEM((2, 128, 64), BF),
            pltpu.VMEM((48, 128), F32),
            pltpu.VMEM((ROWS, 128), BF),
            pltpu.VMEM((HALF, 128), BF),
            pltpu.VMEM((HALF, 128), BF),
            pltpu.VMEM((16, PIECE, 128), BF),
            pltpu.VMEM((PIECE, 128), BF),
            pltpu.VMEM((4, PIECE, 128), BF),
            pltpu.VMEM((PIECE, 128), BF),
            pltpu.VMEM((HALF, 128), BF),
            dma((7,)),
            dma((4,)),
            dma((4,)),
            dma((4,)),
            dma((4,)),
            dma((4,)),
            dma((4,)),
            dma((4,)),
            dma((4,)),
            dma((5,)),
            dma((5,)),
        ],
        compiler_params=pltpu.CompilerParams(
            collective_id=0, has_side_effects=True, vmem_limit_bytes=56 << 20
        ),
    )(
        *(
            array.reshape(2, 64, 1536)
            for array in (
                spatial_queries,
                spatial_keys,
                spatial_values,
                temporal_queries,
                temporal_keys,
                temporal_values,
            )
        ),
        output_gradient.reshape(128, 3072),
        spatial_projection,
        temporal_projection,
        adapter_down.T,
        adapter_up,
        spatial_channel_gate.reshape(1, 3072),
        temporal_channel_gate.reshape(1, 3072),
    )
    outs = pl.pallas_call(
        finish,
        out_shape=(tokens,) * 6
        + (
            jax.ShapeDtypeStruct((64, 1536), F32),
            jax.ShapeDtypeStruct((64, 3072), F32),
            jax.ShapeDtypeStruct((1, 3072), F32),
            jax.ShapeDtypeStruct((1, 3072), F32),
        ),
        in_specs=[pl.BlockSpec(memory_space=pltpu.VMEM)] * 7,
        out_specs=[pl.BlockSpec(memory_space=pltpu.HBM)] * 6
        + [pl.BlockSpec(memory_space=pltpu.VMEM)] * 4,
        scratch_shapes=[dma((6,))],
        compiler_params=pltpu.CompilerParams(vmem_limit_bytes=16 << 20),
    )(*outs)
    return (
        *(array.reshape(1, 2, 64, 1536) for array in outs[:6]),
        outs[6].T,
        outs[7],
        outs[8].reshape(3072),
        outs[9].reshape(3072),
    )


def solution(mesh):
    tokens = P(None, "tm", "space", None)
    return jax.shard_map(
        shards,
        mesh=mesh,
        in_specs=(tokens,) * 7 + (P(),) * 6,
        out_specs=(tokens,) * 6 + (P(),) * 4,
        check_vma=False,
    )
```

```python
import jax
import jax.numpy as jnp
from jax import lax
from jax.experimental import pallas as pl
from jax.experimental.pallas import tpu as pltpu
from jax.sharding import PartitionSpec as P

MESH = pl.DeviceIdType.MESH
BF = jnp.bfloat16
F32 = jnp.float32
SCALE = 128 ** (-0.5)
NN = (((1,), (0,)), ((), ()))
NT = (((1,), (1,)), ((), ()))
TN = (((0,), (0,)), ((), ()))
ROWS = 2560
HALF = 1280
PIECE = 80


def dot(a, b, dims):
    return lax.dot_general(a, b, dims, preferred_element_type=F32)


def aligned(value, unit):
    return pl.multiple_of(value, unit)


def kernel(
    sq, sk, sv, tq, tk, tv, og_hbm, ws_hbm, wt_hbm, down_hbm, up_hbm, gs_hbm, gt_hbm,
    o_sq, o_sk, o_sv, o_tq, o_tk, o_tv, o_down, o_up, o_gs, o_gt,
    sr, so, prob, dsc, tr, to, tprob, og, ws, wt, down, up, gs, gt, gb, glow, ga_s, ga_t, ah_s, ah_t,
    low, gate_rows, pr, r_core, half, r_yz, sum_yz, r_x, sum_x, r_all, r4,
    load_sem, s_in, s_out, t_in, t_out, s_home, s_back, t_home, t_back, red_in, red_out,
):
    t = lax.axis_index("tm")
    s = lax.axis_index("space")
    chip = s // 2
    core = lax.rem(s, 2)
    z = s // 4
    xh = lax.rem(chip, 2)
    xl = t // 4
    y = lax.rem(t, 4)
    plane = y * 4 + z

    loads = [
        pltpu.make_async_copy(src, dst, load_sem.at[n])
        for n, (src, dst) in enumerate(
            ((og_hbm, og), (gs_hbm, gs), (gt_hbm, gt), (up_hbm, up), (down_hbm, down), (ws_hbm, ws), (wt_hbm, wt))
        )
    ]
    for load in loads:
        load.start()

    gate = pltpu.get_barrier_semaphore()

    def greet(device):
        pl.semaphore_signal(gate, inc=1, device_id=device, device_id_type=MESH)

    def greet_space(n, carry):
        greet((t, lax.rem(s + n, 16)))
        return carry

    def greet_tm(n, carry):
        greet((lax.rem(t + n, 8), s))
        return carry

    def greet_plane(n, carry):
        other_y = lax.rem(y + 1 + n // 3, 4)
        other_z = lax.rem(z + 1 + lax.rem(n, 3), 4)
        greet((xl * 4 + other_y, other_z * 4 + xh * 2 + core))
        return carry

    lax.fori_loop(1, 16, greet_space, 0)
    lax.fori_loop(1, 8, greet_tm, 0)
    lax.fori_loop(0, 9, greet_plane, 0)
    greet(((1 - xl) * 4 + y, z * 4 + (1 - xh) * 2 + core))
    pl.semaphore_wait(gate, 32)

    def start_local(src, dst, sem):
        pltpu.make_async_copy(src, dst, sem).start()

    def start_remote(src, dst, send, recv, device):
        pltpu.make_async_remote_copy(
            src, dst, send, recv, device_id=device, device_id_type=MESH
        ).start()

    def await_bytes(ref, sem):
        pltpu.make_async_copy(ref, ref, sem).wait()

    WIDTH = (256, 128)

    def spatial_out(src, i):
        def ends(d, k):
            col = aligned(lax.rem(d, 4) * 384 + k * 256, 128)
            return (
                src.at[d // 4, :, pl.ds(col, WIDTH[k])],
                sr.at[i, pl.ds(aligned(s * 64, 64), 64), pl.ds(0, WIDTH[k])],
            )

        def step(n, carry):
            d = lax.rem(chip + n, 8)
            for k in (0, 1):
                a, b = ends(d, k)
                start_remote(a, b, s_out.at[i], s_in.at[i], (t, d * 2 + k))
            return carry

        lax.fori_loop(1, 8, step, 0)
        for k in (0, 1):
            a, b = ends(chip, k)

            @pl.when(core == k)
            def _():
                start_local(a, b, s_in.at[i])

            @pl.when(core != k)
            def _():
                start_remote(a, b, s_out.at[i], s_in.at[i], (t, chip * 2 + k))

    def spatial_arrived(i):
        @pl.when(core == 0)
        def _():
            await_bytes(sr.at[i], s_in.at[i])

        @pl.when(core == 1)
        def _():
            await_bytes(sr.at[i, :, pl.ds(0, 128)], s_in.at[i])

    def spatial_back(j, home):
        for k in (0, 1):

            @pl.when(core == k)
            def _():
                col = aligned(lax.rem(chip, 4) * 384 + k * 256, 128)
                dst = home.at[chip // 4, :, pl.ds(col, WIDTH[k])]

                def src(d):
                    return so.at[j, pl.ds(aligned(d * 64, 64), 64), pl.ds(0, WIDTH[k])]

                def step(n, carry):
                    d = lax.rem(s + n, 16)
                    start_remote(src(d), dst, s_back.at[j], s_home.at[j], (t, d))
                    return carry

                lax.fori_loop(1, 16, step, 0)
                start_local(src(s), dst, s_home.at[j])

    def temporal_out(src, i):
        def ends(d):
            row = aligned(lax.rem(d, 4) * 16, 16)
            col = aligned((d // 4) * 768, 128)
            return src.at[:, pl.ds(row, 16), pl.ds(col, 768)], tr.at[i, pl.ds(2 * t, 2)]

        def step(n, carry):
            d = lax.rem(t + n, 8)
            a, b = ends(d)
            start_remote(a, b, t_out.at[i], t_in.at[i], (d, s))
            return carry

        lax.fori_loop(1, 8, step, 0)
        a, b = ends(t)
        start_local(a, b, t_in.at[i])

    def temporal_back(j, home):
        row = aligned(lax.rem(t, 4) * 16, 16)
        col = aligned((t // 4) * 768, 128)
        dst = home.at[:, pl.ds(row, 16), pl.ds(col, 768)]

        def step(n, carry):
            d = lax.rem(t + n, 8)
            start_remote(to.at[j, pl.ds(2 * d, 2)], dst, t_back.at[j], t_home.at[j], (d, s))
            return carry

        lax.fori_loop(1, 8, step, 0)
        start_local(to.at[j, pl.ds(2 * t, 2)], dst, t_home.at[j])

    for i, src in enumerate((sq, sk, sv)):
        spatial_out(src, i)

    def attention_gradient(b, channel_gate, weight, weight_load, home):
        branch = (og[...].astype(F32) * channel_gate[...]).astype(BF)
        gb[b] = branch
        small = dot(branch, up[...], NT).astype(BF)
        glow[b] = small
        weight_load.wait()

        def step(n, carry):
            rows = pl.ds(aligned(n * 256, 256), 256)
            part = dot(gb[b], weight[rows, :], NT) + dot(small, down[:, rows], NN)
            home[:, :, rows] = part.astype(BF).reshape(2, 64, 256)
            return carry

        lax.fori_loop(0, 6, step, 0)

    for i, src in enumerate((tq, tk, tv)):
        temporal_out(src, i)
    for load in loads[:5]:
        load.wait()
    attention_gradient(0, gs, ws, loads[5], ga_s)
    attention_gradient(1, gt, wt, loads[6], ga_t)

    heads = 2 - core
    for i in range(3):
        spatial_arrived(i)

    def spatial_forward(h, carry):
        c = pl.ds(aligned(h * 128, 128), 128)
        keys = sr[1, :, c]
        values = sr[2, :, c]
        for n in range(4):
            r = pl.ds(n * 256, 256)
            scores = dot(sr[0, r, c], keys, NT) * SCALE
            expd = jnp.exp(scores - jnp.max(scores, axis=1, keepdims=True))
            total = jnp.sum(expd, axis=1, keepdims=True)
            low_prob = (expd * (1.0 / total)).astype(BF)
            prob[h, r, :] = low_prob
            so[0, r, c] = dot(low_prob, values, NN).astype(BF)
        return carry

    lax.fori_loop(0, heads, spatial_forward, 0)
    spatial_back(0, ah_s)

    def temporal_load(i, h):
        return tr[i, :, :, pl.ds(h * 128, 128)].reshape(256, 128)

    def temporal_store(j, h, value):
        to[j, :, :, pl.ds(h * 128, 128)] = value.astype(BF).reshape(16, 16, 128)

    for i in range(3):
        await_bytes(tr.at[i], t_in.at[i])
    same_patch = lax.rem(lax.broadcasted_iota(jnp.int32, (256, 256), 0), 16) == lax.rem(
        lax.broadcasted_iota(jnp.int32, (256, 256), 1), 16
    )
    for h in range(6):
        scores = dot(temporal_load(0, h), temporal_load(1, h), NT) * SCALE
        scores = jnp.where(same_patch, scores, -1e30)
        expd = jnp.exp(scores - jnp.max(scores, axis=1, keepdims=True))
        total = jnp.sum(expd, axis=1, keepdims=True)
        low_prob = (expd * (1.0 / total)).astype(BF)
        tprob[h] = low_prob
        temporal_store(0, h, dot(low_prob, temporal_load(2, h), NN))
    temporal_back(0, ah_t)

    temporal_out(ga_t, 3)

    spatial_out(ga_s, 3)

    def adapter(b, home, arrived, weight):
        await_bytes(home, arrived)
        rows = home[...].reshape(128, 1536)
        small = dot(rows, down[...], NT).astype(BF)
        low[b] = small

        for n in range(6):
            c = pl.ds(n * 512, 512)
            branch = dot(rows, weight[:, c], NN) + dot(small, up[:, c], NN)
            sums = jnp.sum(og[:, c].astype(F32) * branch, axis=0, keepdims=True)
            for m in range(4):
                gate_rows[pl.ds(b * 24 + n * 4 + m, 1), :] = sums[:, m * 128 : (m + 1) * 128]

    adapter(0, ah_s, s_home.at[0], ws)

    adapter(1, ah_t, t_home.at[0], wt)

    low_st = low[0].astype(F32).T.astype(BF)
    low_tt = low[1].astype(F32).T.astype(BF)
    glow_st = glow[0].astype(F32).T.astype(BF)
    glow_tt = glow[1].astype(F32).T.astype(BF)
    for j in range(24):
        c = pl.ds(j * 128, 128)
        pr[pl.ds(j * 64, 64), :] = (
            dot(low_st, gb[0, :, c], NN) + dot(low_tt, gb[1, :, c], NN)
        ).astype(BF)
    for j in range(12):
        c = pl.ds(j * 128, 128)
        pr[pl.ds(1536 + j * 64, 64), :] = (
            dot(glow_st, ah_s[:, :, c].reshape(128, 128), NN)
            + dot(glow_tt, ah_t[:, :, c].reshape(128, 128), NN)
        ).astype(BF)
    pr[pl.ds(2304, 48), :] = gate_rows[...].astype(BF)
    pr[pl.ds(2352, ROWS - 2352), :] = jnp.zeros((ROWS - 2352, 128), BF)

    other_core = (t, s + 1 - 2 * core)

    def in_plane(j):
        return (xl * 4 + j // 4, lax.rem(j, 4) * 4 + xh * 2 + core)

    def to_plane(stage, src, dst):
        def step(n, carry):
            j = lax.rem(plane + n, 16)
            start_remote(src(j), dst, red_out.at[stage], red_in.at[stage], in_plane(j))
            return carry

        lax.fori_loop(1, 16, step, 0)
        start_local(src(plane), dst, red_in.at[stage])

    start_remote(
        pr.at[pl.ds(aligned((1 - core) * HALF, 16), HALF), :],
        r_core,
        red_out.at[0],
        red_in.at[0],
        other_core,
    )

    await_bytes(tr.at[3], t_in.at[3])
    for h in range(6):
        queries, keys, values, grad = (temporal_load(i, h) for i in range(4))
        attended = to[0, :, :, pl.ds(h * 128, 128)].reshape(256, 128)
        row_dot = jnp.sum(grad.astype(F32) * attended.astype(F32), axis=1, keepdims=True)
        low_prob = tprob[h]
        grad_scores = (low_prob.astype(F32) * (dot(grad, values, NT) - row_dot)).astype(BF)
        temporal_store(1, h, dot(grad_scores, keys, NN) * SCALE)
        temporal_store(2, h, dot(grad_scores, queries, TN) * SCALE)
        temporal_store(3, h, dot(low_prob, grad, TN))

    temporal_back(1, o_tq)

    await_bytes(r_core, red_in.at[0])
    mine = pr[pl.ds(aligned(core * HALF, 16), HALF), :].astype(F32)
    half[...] = (mine + r_core[...].astype(F32)).astype(BF)
    to_plane(1, lambda j: half.at[pl.ds(aligned(j * PIECE, 16), PIECE), :], r_yz.at[plane])

    spatial_arrived(3)

    def spatial_backward(h, carry):
        c = pl.ds(aligned(h * 128, 128), 128)
        keys = sr[1, :, c]
        values = sr[2, :, c]
        for n in range(4):
            r = pl.ds(n * 256, 256)
            grad = sr[3, r, c]
            row_dot = jnp.sum(
                grad.astype(F32) * so[0, r, c].astype(F32), axis=1, keepdims=True
            )
            grad_prob = dot(grad, values, NT)
            grad_scores = (prob[h, r, :].astype(F32) * (grad_prob - row_dot)).astype(BF)
            dsc[r, :] = grad_scores
            so[1, r, c] = (dot(grad_scores, keys, NN) * SCALE).astype(BF)
        queries_t = sr[0, :, c].T
        grads_t = sr[3, :, c].T
        for n in range(4):
            r = pl.ds(n * 256, 256)
            so[2, r, c] = (dot(queries_t, dsc[:, r], NN) * SCALE).T.astype(BF)
            so[3, r, c] = dot(grads_t, prob[h, :, r], NN).T.astype(BF)
        return carry

    lax.fori_loop(0, heads, spatial_backward, 0)

    spatial_back(1, o_sq)

    await_bytes(r_yz, red_in.at[1])
    total = r_yz[0].astype(F32)
    for n in range(1, 16):
        total = total + r_yz[n].astype(F32)
    sum_yz[...] = total.astype(BF)
    slot = r_x.at[xl * 2 + xh]
    for flip_l, flip_h in ((0, 1), (1, 0), (1, 1)):
        device_l = 1 - xl if flip_l else xl
        device_h = 1 - xh if flip_h else xh
        start_remote(
            sum_yz,
            slot,
            red_out.at[2],
            red_in.at[2],
            (device_l * 4 + y, z * 4 + device_h * 2 + core),
        )
    start_local(sum_yz, slot, red_in.at[2])

    temporal_back(2, o_tk)

    spatial_back(2, o_sk)

    spatial_back(3, o_sv)

    temporal_back(3, o_tv)

    await_bytes(r_x, red_in.at[2])
    total = r_x[0].astype(F32)
    for n in range(1, 4):
        total = total + r_x[n].astype(F32)
    sum_x[...] = total.astype(BF)
    to_plane(3, lambda j: sum_x, r_all.at[pl.ds(aligned(plane * PIECE, 16), PIECE), :])

    await_bytes(r_all, red_in.at[3])
    rows = r4.at[pl.ds(aligned(core * HALF, 16), HALF), :]
    start_remote(r_all, rows, red_out.at[4], red_in.at[4], other_core)
    start_local(r_all, rows, red_in.at[4])
    await_bytes(r4, red_in.at[4])

    gates = r4[pl.ds(2304, 48), :].astype(F32)
    for j in range(24):
        c = pl.ds(j * 128, 128)
        o_up[:, c] = r4[pl.ds(j * 64, 64), :].astype(F32)
        o_gs[:, c] = gates[j : j + 1]
        o_gt[:, c] = gates[24 + j : 25 + j]
    for j in range(12):
        o_down[:, pl.ds(j * 128, 128)] = r4[pl.ds(1536 + j * 64, 64), :].astype(F32)

    for j, (s_ref, t_ref) in enumerate(((None, None), (o_sq, o_tq), (o_sk, o_tk), (o_sv, o_tv))):
        if j > 0:
            await_bytes(s_ref, s_home.at[j])
            await_bytes(t_ref, t_home.at[j])
    for i in range(4):
        await_bytes(tr.at[0, pl.ds(0, 14)], t_out.at[i])
        await_bytes(to.at[0, pl.ds(0, 14)], t_back.at[i])
        for k in (0, 1):

            @pl.when(core == k)
            def _():
                await_bytes(og.at[pl.ds(0, 64), pl.ds(0, 3072 - WIDTH[k])], s_out.at[i])
                await_bytes(so.at[0, pl.ds(0, 960), pl.ds(0, WIDTH[k])], s_back.at[i])

    for stage, rows in enumerate((HALF, 15 * PIECE, 3 * PIECE, 15 * PIECE, HALF)):
        await_bytes(pr.at[pl.ds(0, rows), :], red_out.at[stage])


def finish(*refs):
    count = len(refs) // 2
    sem = refs[-1]
    copies = [
        pltpu.make_async_copy(refs[n], refs[count + n], sem.at[n]) for n in range(count)
    ]
    for copy in copies:
        copy.start()
    for copy in copies:
        copy.wait()


def shards(
    spatial_queries,
    spatial_keys,
    spatial_values,
    temporal_queries,
    temporal_keys,
    temporal_values,
    output_gradient,
    spatial_projection,
    temporal_projection,
    adapter_down,
    adapter_up,
    spatial_channel_gate,
    temporal_channel_gate,
):
    results = (((2, 64, 1536), BF),) * 6 + (
        ((64, 1536), F32),
        ((64, 3072), F32),
        ((1, 3072), F32),
        ((1, 3072), F32),
    )
    dma = pltpu.SemaphoreType.DMA
    outs = pl.pallas_call(
        kernel,
        out_shape=tuple(pltpu.VMEM(shape, dtype) for shape, dtype in results),
        in_specs=[pl.BlockSpec(memory_space=pl.ANY)] * 13,
        out_specs=[pl.BlockSpec(memory_space=pl.ANY)] * 6
        + [pl.BlockSpec(memory_space=pltpu.VMEM)] * 4,
        scratch_shapes=[
            pltpu.VMEM((4, 1024, 256), BF),
            pltpu.VMEM((4, 1024, 256), BF),
            pltpu.VMEM((2, 1024, 1024), BF),
            pltpu.VMEM((1024, 1024), BF),
            pltpu.VMEM((4, 16, 16, 768), BF),
            pltpu.VMEM((4, 16, 16, 768), BF),
            pltpu.VMEM((6, 256, 256), BF),
            pltpu.VMEM((128, 3072), BF),
            pltpu.VMEM((1536, 3072), BF),
            pltpu.VMEM((1536, 3072), BF),
            pltpu.VMEM((64, 1536), BF),
            pltpu.VMEM((64, 3072), BF),
            pltpu.VMEM((1, 3072), F32),
            pltpu.VMEM((1, 3072), F32),
            pltpu.VMEM((2, 128, 3072), BF),
            pltpu.VMEM((2, 128, 64), BF),
            pltpu.VMEM((2, 64, 1536), BF),
            pltpu.VMEM((2, 64, 1536), BF),
            pltpu.VMEM((2, 64, 1536), BF),
            pltpu.VMEM((2, 64, 1536), BF),
            pltpu.VMEM((2, 128, 64), BF),
            pltpu.VMEM((48, 128), F32),
            pltpu.VMEM((ROWS, 128), BF),
            pltpu.VMEM((HALF, 128), BF),
            pltpu.VMEM((HALF, 128), BF),
            pltpu.VMEM((16, PIECE, 128), BF),
            pltpu.VMEM((PIECE, 128), BF),
            pltpu.VMEM((4, PIECE, 128), BF),
            pltpu.VMEM((PIECE, 128), BF),
            pltpu.VMEM((HALF, 128), BF),
            pltpu.VMEM((ROWS, 128), BF),
            dma((7,)),
            dma((4,)),
            dma((4,)),
            dma((4,)),
            dma((4,)),
            dma((4,)),
            dma((4,)),
            dma((4,)),
            dma((4,)),
            dma((5,)),
            dma((5,)),
        ],
        compiler_params=pltpu.CompilerParams(
            collective_id=0, has_side_effects=True, vmem_limit_bytes=56 << 20
        ),
    )(
        *(
            array.reshape(2, 64, 1536)
            for array in (
                spatial_queries,
                spatial_keys,
                spatial_values,
                temporal_queries,
                temporal_keys,
                temporal_values,
            )
        ),
        output_gradient.reshape(128, 3072),
        spatial_projection,
        temporal_projection,
        adapter_down.T,
        adapter_up,
        spatial_channel_gate.reshape(1, 3072),
        temporal_channel_gate.reshape(1, 3072),
    )
    outs = pl.pallas_call(
        finish,
        out_shape=tuple(jax.ShapeDtypeStruct(shape, dtype) for shape, dtype in results),
        in_specs=[pl.BlockSpec(memory_space=pltpu.VMEM)] * 10,
        out_specs=[pl.BlockSpec(memory_space=pltpu.HBM)] * 10,
        scratch_shapes=[dma((10,))],
        compiler_params=pltpu.CompilerParams(vmem_limit_bytes=16 << 20),
    )(*outs)
    return (
        *(array.reshape(1, 2, 64, 1536) for array in outs[:6]),
        outs[6].T,
        outs[7],
        outs[8].reshape(3072),
        outs[9].reshape(3072),
    )


def solution(mesh):
    tokens = P(None, "tm", "space", None)
    return jax.shard_map(
        shards,
        mesh=mesh,
        in_specs=(tokens,) * 7 + (P(),) * 6,
        out_specs=(tokens,) * 6 + (P(),) * 4,
        check_vma=False,
    )
```

```python
import jax
import jax.numpy as jnp
from jax import lax
from jax.experimental import pallas as pl
from jax.experimental.pallas import tpu as pltpu
from jax.sharding import PartitionSpec as P

MESH = pl.DeviceIdType.MESH
BF = jnp.bfloat16
F32 = jnp.float32
SCALE = 128 ** (-0.5)
NN = (((1,), (0,)), ((), ()))
NT = (((1,), (1,)), ((), ()))
TN = (((0,), (0,)), ((), ()))
ROWS = 2560
HALF = 1280
PIECE = 80


def dot(a, b, dims):
    return lax.dot_general(a, b, dims, preferred_element_type=F32)


def aligned(value, unit):
    return pl.multiple_of(value, unit)


def kernel(
    sq, sk, sv, tq, tk, tv, og_hbm, ws_hbm, wt_hbm, down_hbm, up_hbm, gs_hbm, gt_hbm,
    o_sq, o_sk, o_sv, o_tq, o_tk, o_tv, o_down, o_up, o_gs, o_gt,
    sr, so, prob, dsc, tr, to, tprob, og, ws, wt, down, up, gs, gt, gb, glow, ga_s, ga_t, ah_s, ah_t,
    low, gate_rows, pr, r_core, half, r_yz, sum_yz, r_x, sum_x, r_all, r4,
    load_sem, s_in, s_out, t_in, t_out, s_home, s_back, t_home, t_back, red_in, red_out,
):
    t = lax.axis_index("tm")
    s = lax.axis_index("space")
    chip = s // 2
    core = lax.rem(s, 2)
    z = s // 4
    xh = lax.rem(chip, 2)
    xl = t // 4
    y = lax.rem(t, 4)
    plane = y * 4 + z

    loads = [
        pltpu.make_async_copy(src, dst, load_sem.at[n])
        for n, (src, dst) in enumerate(
            ((og_hbm, og), (gs_hbm, gs), (gt_hbm, gt), (up_hbm, up), (down_hbm, down), (ws_hbm, ws), (wt_hbm, wt))
        )
    ]
    for load in loads:
        load.start()

    gate = pltpu.get_barrier_semaphore()

    def greet(device):
        pl.semaphore_signal(gate, inc=1, device_id=device, device_id_type=MESH)

    def greet_space(n, carry):
        greet((t, lax.rem(s + n, 16)))
        return carry

    def greet_tm(n, carry):
        greet((lax.rem(t + n, 8), s))
        return carry

    def greet_plane(n, carry):
        other_y = lax.rem(y + 1 + n // 3, 4)
        other_z = lax.rem(z + 1 + lax.rem(n, 3), 4)
        greet((xl * 4 + other_y, other_z * 4 + xh * 2 + core))
        return carry

    lax.fori_loop(1, 16, greet_space, 0)
    lax.fori_loop(1, 8, greet_tm, 0)
    lax.fori_loop(0, 9, greet_plane, 0)
    greet(((1 - xl) * 4 + y, z * 4 + (1 - xh) * 2 + core))
    pl.semaphore_wait(gate, 32)

    def start_local(src, dst, sem):
        pltpu.make_async_copy(src, dst, sem).start()

    def start_remote(src, dst, send, recv, device):
        pltpu.make_async_remote_copy(
            src, dst, send, recv, device_id=device, device_id_type=MESH
        ).start()

    def await_bytes(ref, sem):
        pltpu.make_async_copy(ref, ref, sem).wait()

    WIDTH = (256, 128)

    def spatial_out(src, i):
        def ends(d, k):
            col = aligned(lax.rem(d, 4) * 384 + k * 256, 128)
            return (
                src.at[d // 4, :, pl.ds(col, WIDTH[k])],
                sr.at[i, pl.ds(aligned(s * 64, 64), 64), pl.ds(0, WIDTH[k])],
            )

        def step(n, carry):
            d = lax.rem(chip + n, 8)
            for k in (0, 1):
                a, b = ends(d, k)
                start_remote(a, b, s_out.at[i], s_in.at[i], (t, d * 2 + k))
            return carry

        lax.fori_loop(1, 8, step, 0)
        for k in (0, 1):
            a, b = ends(chip, k)

            @pl.when(core == k)
            def _():
                start_local(a, b, s_in.at[i])

            @pl.when(core != k)
            def _():
                start_remote(a, b, s_out.at[i], s_in.at[i], (t, chip * 2 + k))

    def spatial_arrived(i):
        @pl.when(core == 0)
        def _():
            await_bytes(sr.at[i], s_in.at[i])

        @pl.when(core == 1)
        def _():
            await_bytes(sr.at[i, :, pl.ds(0, 128)], s_in.at[i])

    def spatial_back(j, home):
        for k in (0, 1):

            @pl.when(core == k)
            def _():
                col = aligned(lax.rem(chip, 4) * 384 + k * 256, 128)
                dst = home.at[chip // 4, :, pl.ds(col, WIDTH[k])]

                def src(d):
                    return so.at[j, pl.ds(aligned(d * 64, 64), 64), pl.ds(0, WIDTH[k])]

                def step(n, carry):
                    d = lax.rem(s + n, 16)
                    start_remote(src(d), dst, s_back.at[j], s_home.at[j], (t, d))
                    return carry

                lax.fori_loop(1, 16, step, 0)
                start_local(src(s), dst, s_home.at[j])

    def temporal_out(src, i):
        def ends(d):
            row = aligned(lax.rem(d, 4) * 16, 16)
            col = aligned((d // 4) * 768, 128)
            return src.at[:, pl.ds(row, 16), pl.ds(col, 768)], tr.at[i, pl.ds(2 * t, 2)]

        def step(n, carry):
            d = lax.rem(t + n, 8)
            a, b = ends(d)
            start_remote(a, b, t_out.at[i], t_in.at[i], (d, s))
            return carry

        lax.fori_loop(1, 8, step, 0)
        a, b = ends(t)
        start_local(a, b, t_in.at[i])

    def temporal_back(j, home):
        row = aligned(lax.rem(t, 4) * 16, 16)
        col = aligned((t // 4) * 768, 128)
        dst = home.at[:, pl.ds(row, 16), pl.ds(col, 768)]

        def step(n, carry):
            d = lax.rem(t + n, 8)
            start_remote(to.at[j, pl.ds(2 * d, 2)], dst, t_back.at[j], t_home.at[j], (d, s))
            return carry

        lax.fori_loop(1, 8, step, 0)
        start_local(to.at[j, pl.ds(2 * t, 2)], dst, t_home.at[j])

    for i, src in enumerate((sq, sk, sv)):
        spatial_out(src, i)

    def attention_gradient(b, channel_gate, weight, weight_load, home):
        branch = (og[...].astype(F32) * channel_gate[...]).astype(BF)
        gb[b] = branch
        small = dot(branch, up[...], NT).astype(BF)
        glow[b] = small
        weight_load.wait()

        def step(n, carry):
            rows = pl.ds(aligned(n * 256, 256), 256)
            part = dot(gb[b], weight[rows, :], NT) + dot(small, down[:, rows], NN)
            home[:, :, rows] = part.astype(BF).reshape(2, 64, 256)
            return carry

        lax.fori_loop(0, 6, step, 0)

    for i, src in enumerate((tq, tk, tv)):
        temporal_out(src, i)
    for load in loads[:5]:
        load.wait()
    attention_gradient(0, gs, ws, loads[5], ga_s)
    attention_gradient(1, gt, wt, loads[6], ga_t)

    heads = 2 - core
    for i in range(3):
        spatial_arrived(i)

    def spatial_forward(h, carry):
        c = pl.ds(aligned(h * 128, 128), 128)
        keys = sr[1, :, c]
        values = sr[2, :, c]
        for n in range(4):
            r = pl.ds(n * 256, 256)
            scores = dot(sr[0, r, c], keys, NT) * SCALE
            expd = jnp.exp(scores - jnp.max(scores, axis=1, keepdims=True))
            total = jnp.sum(expd, axis=1, keepdims=True)
            low_prob = (expd * (1.0 / total)).astype(BF)
            prob[h, r, :] = low_prob
            so[0, r, c] = dot(low_prob, values, NN).astype(BF)
        return carry

    lax.fori_loop(0, heads, spatial_forward, 0)
    spatial_back(0, ah_s)

    def temporal_load(i, h):
        return tr[i, :, :, pl.ds(h * 128, 128)].reshape(256, 128)

    def temporal_store(j, h, value):
        to[j, :, :, pl.ds(h * 128, 128)] = value.astype(BF).reshape(16, 16, 128)

    for i in range(3):
        await_bytes(tr.at[i], t_in.at[i])
    same_patch = lax.rem(lax.broadcasted_iota(jnp.int32, (256, 256), 0), 16) == lax.rem(
        lax.broadcasted_iota(jnp.int32, (256, 256), 1), 16
    )
    for h in range(6):
        scores = dot(temporal_load(0, h), temporal_load(1, h), NT) * SCALE
        scores = jnp.where(same_patch, scores, -1e30)
        expd = jnp.exp(scores - jnp.max(scores, axis=1, keepdims=True))
        total = jnp.sum(expd, axis=1, keepdims=True)
        low_prob = (expd * (1.0 / total)).astype(BF)
        tprob[h] = low_prob
        temporal_store(0, h, dot(low_prob, temporal_load(2, h), NN))
    temporal_back(0, ah_t)

    temporal_out(ga_t, 3)

    spatial_out(ga_s, 3)

    def adapter(b, home, arrived, weight):
        await_bytes(home, arrived)
        rows = home[...].reshape(128, 1536)
        small = dot(rows, down[...], NT).astype(BF)
        low[b] = small

        for n in range(6):
            c = pl.ds(n * 512, 512)
            branch = dot(rows, weight[:, c], NN) + dot(small, up[:, c], NN)
            sums = jnp.sum(og[:, c].astype(F32) * branch, axis=0, keepdims=True)
            for m in range(4):
                gate_rows[pl.ds(b * 24 + n * 4 + m, 1), :] = sums[:, m * 128 : (m + 1) * 128]

    adapter(0, ah_s, s_home.at[0], ws)

    adapter(1, ah_t, t_home.at[0], wt)

    low_st = low[0].astype(F32).T.astype(BF)
    low_tt = low[1].astype(F32).T.astype(BF)
    glow_st = glow[0].astype(F32).T.astype(BF)
    glow_tt = glow[1].astype(F32).T.astype(BF)
    for j in range(24):
        c = pl.ds(j * 128, 128)
        pr[pl.ds(j * 64, 64), :] = (
            dot(low_st, gb[0, :, c], NN) + dot(low_tt, gb[1, :, c], NN)
        ).astype(BF)
    for j in range(12):
        c = pl.ds(j * 128, 128)
        pr[pl.ds(1536 + j * 64, 64), :] = (
            dot(glow_st, ah_s[:, :, c].reshape(128, 128), NN)
            + dot(glow_tt, ah_t[:, :, c].reshape(128, 128), NN)
        ).astype(BF)
    pr[pl.ds(2304, 48), :] = gate_rows[...].astype(BF)
    pr[pl.ds(2352, ROWS - 2352), :] = jnp.zeros((ROWS - 2352, 128), BF)

    other_core = (t, s + 1 - 2 * core)

    def in_plane(j):
        return (xl * 4 + j // 4, lax.rem(j, 4) * 4 + xh * 2 + core)

    def to_plane(stage, src, dst):
        def step(n, carry):
            j = lax.rem(plane + n, 16)
            start_remote(src(j), dst, red_out.at[stage], red_in.at[stage], in_plane(j))
            return carry

        lax.fori_loop(1, 16, step, 0)
        start_local(src(plane), dst, red_in.at[stage])

    start_remote(
        pr.at[pl.ds(aligned((1 - core) * HALF, 16), HALF), :],
        r_core,
        red_out.at[0],
        red_in.at[0],
        other_core,
    )

    await_bytes(tr.at[3], t_in.at[3])
    for h in range(6):
        queries, keys, values, grad = (temporal_load(i, h) for i in range(4))
        attended = to[0, :, :, pl.ds(h * 128, 128)].reshape(256, 128)
        row_dot = jnp.sum(grad.astype(F32) * attended.astype(F32), axis=1, keepdims=True)
        low_prob = tprob[h]
        grad_scores = (low_prob.astype(F32) * (dot(grad, values, NT) - row_dot)).astype(BF)
        temporal_store(1, h, dot(grad_scores, keys, NN) * SCALE)
        temporal_store(2, h, dot(grad_scores, queries, TN) * SCALE)
        temporal_store(3, h, dot(low_prob, grad, TN))

    temporal_back(1, o_tq)

    await_bytes(r_core, red_in.at[0])
    mine = pr[pl.ds(aligned(core * HALF, 16), HALF), :].astype(F32)
    half[...] = (mine + r_core[...].astype(F32)).astype(BF)
    to_plane(1, lambda j: half.at[pl.ds(aligned(j * PIECE, 16), PIECE), :], r_yz.at[plane])

    spatial_arrived(3)

    def spatial_backward(h, carry):
        c = pl.ds(aligned(h * 128, 128), 128)
        keys = sr[1, :, c]
        values = sr[2, :, c]
        for n in range(4):
            r = pl.ds(n * 256, 256)
            grad = sr[3, r, c]
            row_dot = jnp.sum(
                grad.astype(F32) * so[0, r, c].astype(F32), axis=1, keepdims=True
            )
            grad_prob = dot(grad, values, NT)
            grad_scores = (prob[h, r, :].astype(F32) * (grad_prob - row_dot)).astype(BF)
            dsc[h, r, :] = grad_scores
            so[1, r, c] = (dot(grad_scores, keys, NN) * SCALE).astype(BF)
        return carry

    lax.fori_loop(0, heads, spatial_backward, 0)
    spatial_back(1, o_sq)

    def spatial_keys_values(h, carry):
        c = pl.ds(aligned(h * 128, 128), 128)
        queries_t = sr[0, :, c].T
        grads_t = sr[3, :, c].T
        for n in range(4):
            r = pl.ds(n * 256, 256)
            so[2, r, c] = (dot(queries_t, dsc[h, :, r], NN) * SCALE).T.astype(BF)
            so[3, r, c] = dot(grads_t, prob[h, :, r], NN).T.astype(BF)
        return carry

    lax.fori_loop(0, heads, spatial_keys_values, 0)


    await_bytes(r_yz, red_in.at[1])
    total = r_yz[0].astype(F32)
    for n in range(1, 16):
        total = total + r_yz[n].astype(F32)
    sum_yz[...] = total.astype(BF)
    slot = r_x.at[xl * 2 + xh]
    for flip_l, flip_h in ((0, 1), (1, 0), (1, 1)):
        device_l = 1 - xl if flip_l else xl
        device_h = 1 - xh if flip_h else xh
        start_remote(
            sum_yz,
            slot,
            red_out.at[2],
            red_in.at[2],
            (device_l * 4 + y, z * 4 + device_h * 2 + core),
        )
    start_local(sum_yz, slot, red_in.at[2])

    temporal_back(2, o_tk)

    spatial_back(2, o_sk)

    spatial_back(3, o_sv)

    temporal_back(3, o_tv)

    await_bytes(r_x, red_in.at[2])
    total = r_x[0].astype(F32)
    for n in range(1, 4):
        total = total + r_x[n].astype(F32)
    sum_x[...] = total.astype(BF)
    to_plane(3, lambda j: sum_x, r_all.at[pl.ds(aligned(plane * PIECE, 16), PIECE), :])

    await_bytes(r_all, red_in.at[3])
    rows = r4.at[pl.ds(aligned(core * HALF, 16), HALF), :]
    start_remote(r_all, rows, red_out.at[4], red_in.at[4], other_core)
    start_local(r_all, rows, red_in.at[4])
    await_bytes(r4, red_in.at[4])

    gates = r4[pl.ds(2304, 48), :].astype(F32)
    for j in range(24):
        c = pl.ds(j * 128, 128)
        o_up[:, c] = r4[pl.ds(j * 64, 64), :].astype(F32)
        o_gs[:, c] = gates[j : j + 1]
        o_gt[:, c] = gates[24 + j : 25 + j]
    for j in range(12):
        o_down[:, pl.ds(j * 128, 128)] = r4[pl.ds(1536 + j * 64, 64), :].astype(F32)

    for j, (s_ref, t_ref) in enumerate(((None, None), (o_sq, o_tq), (o_sk, o_tk), (o_sv, o_tv))):
        if j > 0:
            await_bytes(s_ref, s_home.at[j])
            await_bytes(t_ref, t_home.at[j])
    for i in range(4):
        await_bytes(tr.at[0, pl.ds(0, 14)], t_out.at[i])
        await_bytes(to.at[0, pl.ds(0, 14)], t_back.at[i])
        for k in (0, 1):

            @pl.when(core == k)
            def _():
                await_bytes(og.at[pl.ds(0, 64), pl.ds(0, 3072 - WIDTH[k])], s_out.at[i])
                await_bytes(so.at[0, pl.ds(0, 960), pl.ds(0, WIDTH[k])], s_back.at[i])

    for stage, rows in enumerate((HALF, 15 * PIECE, 3 * PIECE, 15 * PIECE, HALF)):
        await_bytes(pr.at[pl.ds(0, rows), :], red_out.at[stage])


def finish(*refs):
    count = len(refs) // 2
    sem = refs[-1]
    copies = [
        pltpu.make_async_copy(refs[n], refs[count + n], sem.at[n]) for n in range(count)
    ]
    for copy in copies:
        copy.start()
    for copy in copies:
        copy.wait()


def shards(
    spatial_queries,
    spatial_keys,
    spatial_values,
    temporal_queries,
    temporal_keys,
    temporal_values,
    output_gradient,
    spatial_projection,
    temporal_projection,
    adapter_down,
    adapter_up,
    spatial_channel_gate,
    temporal_channel_gate,
):
    results = (((2, 64, 1536), BF),) * 6 + (
        ((64, 1536), F32),
        ((64, 3072), F32),
        ((1, 3072), F32),
        ((1, 3072), F32),
    )
    dma = pltpu.SemaphoreType.DMA
    outs = pl.pallas_call(
        kernel,
        out_shape=tuple(pltpu.VMEM(shape, dtype) for shape, dtype in results),
        in_specs=[pl.BlockSpec(memory_space=pl.ANY)] * 13,
        out_specs=[pl.BlockSpec(memory_space=pl.ANY)] * 6
        + [pl.BlockSpec(memory_space=pltpu.VMEM)] * 4,
        scratch_shapes=[
            pltpu.VMEM((4, 1024, 256), BF),
            pltpu.VMEM((4, 1024, 256), BF),
            pltpu.VMEM((2, 1024, 1024), BF),
            pltpu.VMEM((2, 1024, 1024), BF),
            pltpu.VMEM((4, 16, 16, 768), BF),
            pltpu.VMEM((4, 16, 16, 768), BF),
            pltpu.VMEM((6, 256, 256), BF),
            pltpu.VMEM((128, 3072), BF),
            pltpu.VMEM((1536, 3072), BF),
            pltpu.VMEM((1536, 3072), BF),
            pltpu.VMEM((64, 1536), BF),
            pltpu.VMEM((64, 3072), BF),
            pltpu.VMEM((1, 3072), F32),
            pltpu.VMEM((1, 3072), F32),
            pltpu.VMEM((2, 128, 3072), BF),
            pltpu.VMEM((2, 128, 64), BF),
            pltpu.VMEM((2, 64, 1536), BF),
            pltpu.VMEM((2, 64, 1536), BF),
            pltpu.VMEM((2, 64, 1536), BF),
            pltpu.VMEM((2, 64, 1536), BF),
            pltpu.VMEM((2, 128, 64), BF),
            pltpu.VMEM((48, 128), F32),
            pltpu.VMEM((ROWS, 128), BF),
            pltpu.VMEM((HALF, 128), BF),
            pltpu.VMEM((HALF, 128), BF),
            pltpu.VMEM((16, PIECE, 128), BF),
            pltpu.VMEM((PIECE, 128), BF),
            pltpu.VMEM((4, PIECE, 128), BF),
            pltpu.VMEM((PIECE, 128), BF),
            pltpu.VMEM((HALF, 128), BF),
            pltpu.VMEM((ROWS, 128), BF),
            dma((7,)),
            dma((4,)),
            dma((4,)),
            dma((4,)),
            dma((4,)),
            dma((4,)),
            dma((4,)),
            dma((4,)),
            dma((4,)),
            dma((5,)),
            dma((5,)),
        ],
        compiler_params=pltpu.CompilerParams(
            collective_id=0, has_side_effects=True, vmem_limit_bytes=56 << 20
        ),
    )(
        *(
            array.reshape(2, 64, 1536)
            for array in (
                spatial_queries,
                spatial_keys,
                spatial_values,
                temporal_queries,
                temporal_keys,
                temporal_values,
            )
        ),
        output_gradient.reshape(128, 3072),
        spatial_projection,
        temporal_projection,
        adapter_down.T,
        adapter_up,
        spatial_channel_gate.reshape(1, 3072),
        temporal_channel_gate.reshape(1, 3072),
    )
    outs = pl.pallas_call(
        finish,
        out_shape=tuple(jax.ShapeDtypeStruct(shape, dtype) for shape, dtype in results),
        in_specs=[pl.BlockSpec(memory_space=pltpu.VMEM)] * 10,
        out_specs=[pl.BlockSpec(memory_space=pltpu.HBM)] * 10,
        scratch_shapes=[dma((10,))],
        compiler_params=pltpu.CompilerParams(vmem_limit_bytes=16 << 20),
    )(*outs)
    return (
        *(array.reshape(1, 2, 64, 1536) for array in outs[:6]),
        outs[6].T,
        outs[7],
        outs[8].reshape(3072),
        outs[9].reshape(3072),
    )


def solution(mesh):
    tokens = P(None, "tm", "space", None)
    return jax.shard_map(
        shards,
        mesh=mesh,
        in_specs=(tokens,) * 7 + (P(),) * 6,
        out_specs=(tokens,) * 6 + (P(),) * 4,
        check_vma=False,
    )
```
